32 devices in a mesh: dp: 4 (over y, x), ctx: 2 (over core), exp: 4 (over z).
Axes of the slice: x: 2, y: 2, z: 4, core: 2. Of those that a mesh axis runs over, the one named last changes fastest.
Arguments:
- queries: bfloat16 [4, 256, 16, 576], P('dp', 'ctx', 'exp'), may hold values from -7 to 7
- out_grad: bfloat16 [4, 256, 16, 512], P('dp', 'ctx', 'exp'), may hold values from -6 to 6
- latent_keys: bfloat16 [4, 256, 576], P('dp', 'ctx'), may hold values from -9 to 9
- kv_gain: float32 [512], replicated, may hold values from 0.5 to 2
- query_groups: int32 [4, 2], P('dp'), may hold values from 0 to 1, each once within a row
Outputs:
- grad_queries: bfloat16 [4, 256, 16, 576], P('dp', 'ctx', 'exp')
- grad_keys: float32 [4, 2, 128, 576], P('dp', 'ctx', 'exp')
- grad_gain: float32 [512], replicated
The draws below stay inside these ranges and needn't reach their ends.
Inputs may be any that keep to these rules, and one draw needn't show every extreme that they name: `query_groups`: each row names each group index once.
All inputs are finite; a program needn't handle non-finite values.
Results may differ from the reference program's by a relative error of at most 0.0049.
Values may be sent and summed in bfloat16 or wider, within the bound.
No kernel may reach another device: no remote copies, remote signals or barrier semaphores. Data moves between devices by JAX's collectives and lax.ppermute only.
A program may use at most 64 MiB of HBM per device.

```python
import math
import jax
import jax.numpy as jnp
from jax import lax

LATENT = 512
ROPE = 64
GROUP = 128
HEADS = 16
BATCH = 4
QUERIES = 256
KEYS = 256
N_CTX = 2


def key_table(key, scale_low, scale_high, gap_size):
    key_width = LATENT + ROPE
    shape = (BATCH, KEYS, key_width)
    normal_part = jnp.clip(jax.random.normal(jax.random.fold_in(key, 1), shape, jnp.float32), -4.0, 4.0)
    key_rows = normal_part
    row_scale = jnp.exp(jax.random.uniform(jax.random.fold_in(key, 3), (BATCH, KEYS, 1), jnp.float32, math.log(scale_low), math.log(scale_high)))
    row_ids = jnp.arange(KEYS)[None, :, None]
    key_rows = jnp.where(row_ids < 2, key_rows, key_rows * row_scale)
    column_ids = jnp.arange(key_width)[None, None, :]
    first_row = key_rows[:, 0:1, :]
    lead_row = jnp.where(column_ids < 8, 1.0, first_row)
    twin_row = jnp.where(column_ids < 8, 1.0 - gap_size, first_row)
    key_rows = jnp.where(row_ids == 0, lead_row, jnp.where(row_ids == 1, twin_row, key_rows))
    return key_rows


def draw_latent_keys(key, part):
    key_rows = key_table(key, 1.0, 1.0, 0.74)
    return key_rows.astype(jnp.bfloat16)


def draw_queries(key, part):
    key = jax.random.fold_in(key, 5)
    full_shape = (BATCH, QUERIES, HEADS, LATENT + ROPE)
    values_drawn = jnp.clip(jax.random.normal(jax.random.fold_in(key, 1), full_shape, jnp.float32), -4.0, 4.0) * 0.3
    return values_drawn.astype(jnp.bfloat16)


def block_levels(rng, shape, cuts, smallest, top_value):
    level = 1.0
    for dim, parts in cuts:
        draws = jax.random.uniform(jax.random.fold_in(jax.random.fold_in(rng, 6), dim), (parts,), jnp.float32, smallest / len(cuts), top_value / len(cuts))
        level = level * jnp.repeat(jnp.exp(draws), shape[dim] // parts).reshape((-1,) + (1,) * (len(shape) - 1 - dim))
    return level


def bell_draw(key, dims, scale, limit, split=(), kind=jnp.bfloat16):
    factor_of = block_levels(key, dims, split, -0.22, 0.18) if split else 1.0
    array = jax.random.normal(key, dims, jnp.float32) * scale * factor_of
    return jnp.minimum(jnp.maximum(array, -limit), limit).astype(kind)


def setup_inputs(seed: int = 0) -> dict:
    seeds = jax.random.split(jax.random.key(seed), 6)
    return {
        "queries": draw_queries(jax.random.fold_in(seeds[5], 71), 0),
        "out_grad": bell_draw(seeds[1], (BATCH, QUERIES, HEADS, LATENT), 1.0, 6.0, ((0, 4), (1, 2), (2, 4))),
        "latent_keys": draw_latent_keys(jax.random.fold_in(seeds[5], 71), 0),
        "kv_gain": jnp.clip(jnp.exp(jax.random.uniform(seeds[3], (LATENT,), jnp.float32, math.log(0.5), math.log(2.0))), 0.5, 2.0),
        "query_groups": jax.vmap(lambda own: jax.random.permutation(own, N_CTX))(jax.random.split(seeds[4], BATCH)).reshape((BATCH, N_CTX)).astype(jnp.int32),
    }


SOFTMAX_SCALE = (0.1 * math.log(40.0) + 1.0) ** 2 / math.sqrt(192.0)
MASKED_SCORE = -1e+30

def one_sequence(queries, out_grad, latent_keys, visible):
    key_width = LATENT + ROPE
    values = latent_keys[:, :LATENT]

    def one_head(running, inputs):
        query_rows, grad_rows = inputs
        scores = jnp.dot(query_rows, latent_keys.T, preferred_element_type=jnp.float32) * SOFTMAX_SCALE
        scores = jnp.where(visible, scores, MASKED_SCORE)
        row_max = lax.optimization_barrier(jnp.max(scores, axis=1))
        exponent = jnp.where(visible, jnp.exp(scores - row_max[:, None]), 0.0)
        weights = exponent / lax.optimization_barrier(jnp.sum(exponent, axis=1))[:, None]
        grad_prob = jnp.dot(grad_rows, values.T, preferred_element_type=jnp.float32)
        row_delta = lax.optimization_barrier(jnp.sum(weights * grad_prob, axis=1))
        dscore = (weights * (grad_prob - row_delta[:, None])).astype(jnp.bfloat16)
        weights_low = weights.astype(jnp.bfloat16)
        grad_query = (jnp.dot(dscore, latent_keys, preferred_element_type=jnp.float32) * SOFTMAX_SCALE).astype(jnp.bfloat16)
        key_part = jnp.dot(dscore.T, query_rows, preferred_element_type=jnp.float32) * SOFTMAX_SCALE
        value_part = jnp.dot(weights_low.T, grad_rows, preferred_element_type=jnp.float32)
        key_part = key_part + jnp.pad(value_part, ((0, 0), (0, ROPE)))
        return (running + key_part, grad_query)
    initial = jnp.zeros((KEYS, key_width), jnp.float32)
    grad_keys, grad_heads = lax.scan(one_head, initial, (jnp.swapaxes(queries, 0, 1), jnp.swapaxes(out_grad, 0, 1)))
    return (jnp.swapaxes(grad_heads, 0, 1), grad_keys)

def reference(queries, out_grad, latent_keys, kv_gain, query_groups):
    key_width = LATENT + ROPE
    offsets = jnp.arange(GROUP, dtype=jnp.int32)
    key_pos = jnp.arange(KEYS, dtype=jnp.int32)

    def per_sequence(inputs):
        group_row = inputs[3].astype(jnp.int32)
        query_pos = (group_row[:, None] * GROUP + offsets[None, :]).reshape(-1)
        visible = key_pos[None, :] <= query_pos[:, None]
        return one_sequence(inputs[0], inputs[1], inputs[2], visible)
    grad_queries, grad_keys = lax.map(per_sequence, (queries, out_grad, latent_keys, query_groups))
    products = grad_keys[:, :, :LATENT] * latent_keys[:, :, :LATENT].astype(jnp.float32)
    grad_gain = lax.optimization_barrier(jnp.sum(products, axis=(0, 1))) / kv_gain
    return (grad_queries, grad_keys.reshape(BATCH, N_CTX, GROUP, key_width), grad_gain)
```

```python
import math

import jax
import jax.numpy as jnp
from jax import lax
from jax.experimental import pallas as pl
from jax.experimental.pallas import tpu as pltpu
from jax.sharding import PartitionSpec as P

LATENT = 512
SOFTMAX_SCALE = (0.1 * math.log(40.0) + 1.0) ** 2 / math.sqrt(192.0)
MASKED_SCORE = -1e30
TAIL = 64
TAIL_ROWS = LATENT // TAIL

NT = (((1,), (1,)), ((), ()))
F32, BF16 = jnp.float32, jnp.bfloat16


def shift(value, axis, step):
    size = lax.axis_size(axis)
    return lax.ppermute(value, axis, [(i, (i - step) % size) for i in range(size)])


EXP_STEPS = ((2, 3, 1, 0), (3, 2, 0, 1), (1, 0, 3, 2))
DP_STEPS = ((1, 3, 0, 2), (2, 0, 3, 1), (3, 2, 1, 0))


def exchange_steps(steps, size):
    if size == 4:
        return steps
    return tuple(tuple((i + k) % size for i in range(size)) for k in range(1, size))


def target_of(place, step):
    size = len(step)
    if size != 4:
        return lax.rem(place + step[0], size)
    target = jnp.int32(step[0])
    for i in range(1, size):
        target = jnp.where(place == i, step[i], target)
    return target


def send_step(value, axis, step):
    return lax.ppermute(value, axis, list(enumerate(step)))


def dot(a, b):
    return jnp.dot(a, b, preferred_element_type=F32)


def dot_nt(a, b):
    return lax.dot_general(a, b, NT, preferred_element_type=F32)


def gain_tail(gain):
    high = gain.astype(BF16).astype(F32)
    return jnp.concatenate(
        [
            part[:, r * TAIL : (r + 1) * TAIL]
            for part in (high, gain - high)
            for r in range(TAIL_ROWS)
        ],
        axis=0,
    ).astype(BF16)


def tail_gain(tail):
    tail = tail[:TAIL_ROWS] + tail[TAIL_ROWS:]
    return jnp.concatenate([tail[r : r + 1] for r in range(TAIL_ROWS)], axis=1)


def write_tail(ref, tail):
    rows, width = ref.shape
    if rows > 2 * TAIL_ROWS:
        ref[2 * TAIL_ROWS :, width - TAIL :] = jnp.zeros((rows - 2 * TAIL_ROWS, TAIL), BF16)
    ref[: 2 * TAIL_ROWS, width - TAIL :] = tail


def block_scores(keys, queries_t, grads, first_key, query_pos):
    scores = dot(keys, queries_t) * SOFTMAX_SCALE
    grad_prob = dot_nt(keys[:, :LATENT], grads)
    key_pos = first_key + lax.broadcasted_iota(jnp.int32, scores.shape, 0)
    return jnp.where(key_pos <= query_pos, scores, MASKED_SCORE), grad_prob


def own_scores_kernel(
    groups_hbm, kv_gain_hbm, q_hbm, g_hbm, key_hbm,
    queries_ref, grads_ref, keys_ref, scores_ref, grad_prob_ref, query_pos_ref, kv_gain_ref,
    groups, g_ref, key_ref, copied,
):
    heads, _, rows_q = q_hbm.shape
    rows_k = key_ref.shape[1]
    q_copies = [
        pltpu.make_async_copy(
            q_hbm.at[h], queries_ref.at[:, pl.ds(h * rows_q, rows_q)], copied.at[4 + h]
        )
        for h in range(heads)
    ]
    key_copy = pltpu.make_async_copy(key_hbm, key_ref, copied.at[0])
    groups_copy = pltpu.make_async_copy(groups_hbm, groups, copied.at[1])
    g_copy = pltpu.make_async_copy(g_hbm, g_ref, copied.at[2])
    gain_copy = pltpu.make_async_copy(kv_gain_hbm, kv_gain_ref, copied.at[3])
    for copy in (key_copy, groups_copy, g_copy, *q_copies, gain_copy):
        copy.start()

    key_copy.wait()
    keys = key_ref[...].T
    keys_ref[...] = keys
    g_copy.wait()
    grads = jnp.swapaxes(g_ref[...], 0, 1).reshape(heads * rows_q, LATENT)
    grads_ref[...] = grads
    groups_copy.wait()
    place = lax.axis_index("ctx")
    query_pos = groups[0, place] * rows_q + lax.rem(
        lax.broadcasted_iota(jnp.int32, (1, heads * rows_q), 1), rows_q
    )
    query_pos_ref[...] = query_pos
    for copy in q_copies:
        copy.wait()
    scores_ref[...], grad_prob_ref[...] = block_scores(
        keys, queries_ref[...], grads, place * rows_k, query_pos
    )
    gain_copy.wait()


def softmax_kernel(ctx_count, *refs):
    queries_ref, grads_ref, keys_ref, scores_ref, grad_prob_ref, query_pos_ref = refs[:6]
    peer_refs = refs[6 : 5 + ctx_count]
    dscore_ref, own_ref, gain_ref = refs[5 + ctx_count : 8 + ctx_count]
    send_refs = refs[8 + ctx_count :]
    rows_k = keys_ref.shape[0]
    place = lax.axis_index("ctx")
    queries_t = queries_ref[...]
    grads = grads_ref[...]

    keys = [keys_ref[...]] + [ref[...].T for ref in peer_refs]
    blocks = [(scores_ref[...], grad_prob_ref[...])]
    for b in range(1, ctx_count):
        first_key = lax.rem(place + b, ctx_count) * rows_k
        blocks.append(block_scores(keys[b], queries_t, grads, first_key, query_pos_ref[...]))
    scores = jnp.concatenate([block[0] for block in blocks], axis=0)
    grad_prob = jnp.concatenate([block[1] for block in blocks], axis=0)
    row_max = jnp.max(scores, axis=0, keepdims=True)
    exponent = jnp.where(scores > MASKED_SCORE, jnp.exp(scores - row_max), 0.0)
    weights = exponent * (1.0 / jnp.sum(exponent, axis=0, keepdims=True))
    row_delta = jnp.sum(weights * grad_prob, axis=0, keepdims=True)
    dscore = (weights * (grad_prob - row_delta)).astype(BF16)
    weights_low = weights.astype(BF16)
    dscore_ref[...] = dscore

    key_part = dot_nt(dscore, queries_t) * SOFTMAX_SCALE
    latent_part = key_part[:, :LATENT] + dot(weights_low, grads)
    all_keys = jnp.concatenate(keys, axis=0)[:, :LATENT]
    gain = jnp.sum(latent_part * all_keys.astype(F32), axis=0, keepdims=True)
    gain_ref[...] = gain
    tail = gain_tail(gain)
    width = key_part.shape[1]
    for b in range(ctx_count):
        rows = slice(b * rows_k, (b + 1) * rows_k)
        target = own_ref if b == 0 else send_refs[b - 1]
        target[:, :LATENT] = latent_part[rows].astype(target.dtype)
        target[:, LATENT:width] = key_part[rows, LATENT:].astype(target.dtype)
        if b:
            write_tail(target, tail)


def grad_queries_kernel(*refs):
    dscore_ref, *key_refs, dq_ref = refs
    heads, _, rows_q = dq_ref.shape
    keys_t = jnp.concatenate([ref[...] for ref in key_refs], axis=1)
    dq_t = dot(keys_t, dscore_ref[...]) * SOFTMAX_SCALE
    for h in range(heads):
        dq_ref[h] = dq_t[:, h * rows_q : (h + 1) * rows_q].astype(BF16)


def pair_kernel(ctx_count, exp_count, *refs):
    own_ref, gain_ref = refs[:2]
    recv_refs = refs[2 : 1 + ctx_count]
    kept_ref, gain_out = refs[1 + ctx_count : 3 + ctx_count]
    send_refs = refs[3 + ctx_count : -1]
    total = refs[-1]
    share, width = kept_ref.shape
    value = own_ref[...]
    gain = gain_ref[...]
    for ref in recv_refs:
        value = value + ref[:, :width].astype(F32)
        gain = gain + tail_gain(ref[: 2 * TAIL_ROWS, width:].astype(F32))
    total[...] = value.reshape(total.shape)
    gain_out[...] = gain
    tail = gain_tail(gain)
    place = lax.axis_index("exp")
    kept_ref[...] = total[place]
    for step, ref in zip(exchange_steps(EXP_STEPS, exp_count), send_refs):
        if ref.shape[0] > share:
            ref[...] = jnp.zeros(ref.shape, ref.dtype)
        ref[:share, :width] = total[target_of(place, step)].astype(BF16)
        write_tail(ref, tail)


def gain_kernel(*refs):
    gain_ref, *recv_refs, gain_out = refs
    tail = jnp.zeros((2 * TAIL_ROWS, TAIL), F32)
    for ref in recv_refs:
        tail = tail + ref[: 2 * TAIL_ROWS, ref.shape[1] - TAIL :].astype(F32)
    gain_out[...] = gain_ref[...] + tail_gain(tail)


def final_kernel(gain_count, *refs):
    gain_refs = refs[:gain_count]
    kv_gain_ref, kept_ref, *recv_refs, out_ref, gain_out = refs[gain_count:]
    share, width = kept_ref.shape
    rows = kept_ref[...]
    for ref in recv_refs:
        rows = rows + ref[:share, :width].astype(F32)
    out_ref[...] = rows
    gain = gain_refs[0][...]
    for ref in gain_refs[1:]:
        gain = gain + ref[...]
    gain_out[...] = gain / kv_gain_ref[...]


def call(kernel, out_shapes, operands, flops, scratch=(), fetch=False):
    space = pl.ANY if fetch else pltpu.VMEM
    size = sum(x.size * x.dtype.itemsize for x in (*operands, *out_shapes))
    if fetch:
        out_shapes = [pltpu.VMEM(x.shape, x.dtype) for x in out_shapes]
    return pl.pallas_call(
        kernel,
        out_shape=list(out_shapes),
        in_specs=[pl.BlockSpec(memory_space=space)] * len(operands),
        out_specs=[pl.BlockSpec(memory_space=pltpu.VMEM)] * len(out_shapes),
        scratch_shapes=list(scratch),
        compiler_params=pltpu.CompilerParams(vmem_limit_bytes=(56 if fetch else 48) * 2**20),
        cost_estimate=pl.CostEstimate(flops=flops, bytes_accessed=size, transcendentals=0),
    )(*operands)


def body(queries, out_grad, latent_keys, kv_gain, query_groups):
    ctx_count = lax.axis_size("ctx")
    exp_count = lax.axis_size("exp")
    _, rows_q, heads, width = queries.shape
    rows_k = latent_keys.shape[1]
    share = rows_k // exp_count
    keys_all = rows_k * ctx_count
    rows_all = rows_q * heads
    both = width + LATENT

    def f32(*shape):
        return jax.ShapeDtypeStruct(shape, F32)

    def bf16(*shape):
        return jax.ShapeDtypeStruct(shape, BF16)

    own_keys = latent_keys[0].T
    peer_keys = [shift(own_keys, "ctx", b) for b in range(1, ctx_count)]

    *prepared, query_pos, kv_gain_row = call(
        own_scores_kernel,
        [
            bf16(width, rows_all),
            bf16(rows_all, LATENT),
            bf16(rows_k, width),
            f32(rows_k, rows_all),
            f32(rows_k, rows_all),
            jax.ShapeDtypeStruct((1, rows_all), jnp.int32),
            f32(1, LATENT),
        ],
        [
            query_groups,
            kv_gain.reshape(1, LATENT),
            jnp.transpose(queries[0], (1, 2, 0)),
            out_grad[0],
            own_keys,
        ],
        2 * rows_all * rows_k * both,
        [
            pltpu.SMEM(query_groups.shape, jnp.int32),
            pltpu.VMEM((rows_q, heads, LATENT), BF16),
            pltpu.VMEM((width, rows_k), BF16),
            pltpu.SemaphoreType.DMA((4 + heads,)),
        ],
        fetch=True,
    )
    dscore, own, gain, *sends = call(
        lambda *refs: softmax_kernel(ctx_count, *refs),
        [bf16(keys_all, rows_all), f32(rows_k, width), f32(1, LATENT)]
        + [bf16(rows_k, width + TAIL)] * (ctx_count - 1),
        [*prepared, query_pos, *peer_keys],
        2 * rows_all * (2 * keys_all - rows_k) * both,
    )
    received = [shift(sends[b - 1], "ctx", -b) for b in range(1, ctx_count)]
    (dq_t,) = call(
        grad_queries_kernel,
        [bf16(heads, width, rows_q)],
        [dscore, own_keys, *peer_keys],
        2 * rows_all * keys_all * width,
    )
    message = bf16(max(share, 2 * TAIL_ROWS), width + TAIL)
    exp_steps = exchange_steps(EXP_STEPS, exp_count)
    kept, gain, *sends = call(
        lambda *refs: pair_kernel(ctx_count, exp_count, *refs),
        [f32(share, width), f32(1, LATENT)] + [message] * len(exp_steps),
        [own, gain, *received],
        rows_k * width * ctx_count,
        [pltpu.VMEM((exp_count, share, width), F32)],
    )
    received = [send_step(send, "exp", step) for send, step in zip(sends, exp_steps)]
    (gain,) = call(gain_kernel, [f32(1, LATENT)], [gain, *received], LATENT * exp_count)
    gains = [gain] + [
        send_step(gain, "dp", step)
        for step in reversed(exchange_steps(DP_STEPS, lax.axis_size("dp")))
    ]
    grad_keys, grad_gain = call(
        lambda *refs: final_kernel(len(gains), *refs),
        [f32(share, width), f32(1, LATENT)],
        [*gains, kv_gain_row, kept, *received],
        share * width * exp_count,
    )
    grad_queries = jnp.transpose(dq_t, (2, 0, 1))[None]
    return (grad_queries, grad_keys[None, None], grad_gain.reshape(LATENT))


def solution(mesh):
    in_specs = (
        P("dp", "ctx", "exp", None),
        P("dp", "ctx", "exp", None),
        P("dp", "ctx", None),
        P(),
        P("dp", None),
    )
    out_specs = (P("dp", "ctx", "exp", None), P("dp", "ctx", "exp", None), P())
    return jax.shard_map(body, mesh=mesh, in_specs=in_specs, out_specs=out_specs, check_vma=False)
```

```python
import math

import jax
import jax.numpy as jnp
from jax import lax
from jax.experimental import pallas as pl
from jax.experimental.pallas import tpu as pltpu
from jax.sharding import PartitionSpec as P

LATENT = 512
SOFTMAX_SCALE = (0.1 * math.log(40.0) + 1.0) ** 2 / math.sqrt(192.0)
MASKED_SCORE = -1e30
TAIL = 64
TAIL_ROWS = LATENT // TAIL

NT = (((1,), (1,)), ((), ()))
F32, BF16 = jnp.float32, jnp.bfloat16


def shift(value, axis, step):
    size = lax.axis_size(axis)
    return lax.ppermute(value, axis, [(i, (i - step) % size) for i in range(size)])


EXP_STEPS = ((2, 3, 1, 0), (3, 2, 0, 1), (1, 0, 3, 2))
DP_STEPS = ((1, 3, 0, 2), (2, 0, 3, 1), (3, 2, 1, 0))


def exchange_steps(steps, size):
    if size == 4:
        return steps
    return tuple(tuple((i + k) % size for i in range(size)) for k in range(1, size))


def target_of(place, step):
    size = len(step)
    if size != 4:
        return lax.rem(place + step[0], size)
    target = jnp.int32(step[0])
    for i in range(1, size):
        target = jnp.where(place == i, step[i], target)
    return target


def send_step(value, axis, step):
    return lax.ppermute(value, axis, list(enumerate(step)))


def dot(a, b):
    return jnp.dot(a, b, preferred_element_type=F32)


def dot_nt(a, b):
    return lax.dot_general(a, b, NT, preferred_element_type=F32)


def gain_tail(gain):
    high = gain.astype(BF16).astype(F32)
    return jnp.concatenate(
        [
            part[:, r * TAIL : (r + 1) * TAIL]
            for part in (high, gain - high)
            for r in range(TAIL_ROWS)
        ],
        axis=0,
    ).astype(BF16)


def tail_gain(tail):
    tail = tail[:TAIL_ROWS] + tail[TAIL_ROWS:]
    return jnp.concatenate([tail[r : r + 1] for r in range(TAIL_ROWS)], axis=1)


def write_tail(ref, tail):
    rows, width = ref.shape
    if rows > 2 * TAIL_ROWS:
        ref[2 * TAIL_ROWS :, width - TAIL :] = jnp.zeros((rows - 2 * TAIL_ROWS, TAIL), BF16)
    ref[: 2 * TAIL_ROWS, width - TAIL :] = tail


def block_scores(keys, queries_t, grads, first_key, query_pos):
    scores = dot(keys, queries_t) * SOFTMAX_SCALE
    grad_prob = dot_nt(keys[:, :LATENT], grads)
    key_pos = first_key + lax.broadcasted_iota(jnp.int32, scores.shape, 0)
    return jnp.where(key_pos <= query_pos, scores, MASKED_SCORE), grad_prob


def own_scores_kernel(
    groups_hbm, kv_gain_hbm, q_hbm, g_hbm, key_hbm,
    queries_ref, grads_ref, keys_ref, scores_ref, grad_prob_ref, query_pos_ref, kv_gain_ref,
    groups, g_ref, key_ref, copied,
):
    heads, _, rows_q = q_hbm.shape
    rows_k = key_ref.shape[1]
    q_copies = [
        pltpu.make_async_copy(
            q_hbm.at[h], queries_ref.at[:, pl.ds(h * rows_q, rows_q)], copied.at[4 + h]
        )
        for h in range(heads)
    ]
    key_copy = pltpu.make_async_copy(key_hbm, key_ref, copied.at[0])
    groups_copy = pltpu.make_async_copy(groups_hbm, groups, copied.at[1])
    g_copy = pltpu.make_async_copy(g_hbm, g_ref, copied.at[2])
    gain_copy = pltpu.make_async_copy(kv_gain_hbm, kv_gain_ref, copied.at[3])
    for copy in (key_copy, groups_copy, g_copy, *q_copies, gain_copy):
        copy.start()

    key_copy.wait()
    keys = key_ref[...].T
    keys_ref[...] = keys
    g_copy.wait()
    grads = jnp.swapaxes(g_ref[...], 0, 1).reshape(heads * rows_q, LATENT)
    grads_ref[...] = grads
    groups_copy.wait()
    place = lax.axis_index("ctx")
    query_pos = groups[0, place] * rows_q + lax.rem(
        lax.broadcasted_iota(jnp.int32, (1, heads * rows_q), 1), rows_q
    )
    query_pos_ref[...] = query_pos
    for copy in q_copies:
        copy.wait()
    scores_ref[...], grad_prob_ref[...] = block_scores(
        keys, queries_ref[...], grads, place * rows_k, query_pos
    )
    gain_copy.wait()


def softmax_kernel(ctx_count, *refs):
    queries_ref, grads_ref, keys_ref, scores_ref, grad_prob_ref, query_pos_ref = refs[:6]
    peer_refs = refs[6 : 5 + ctx_count]
    dscore_ref, own_ref, gain_ref = refs[5 + ctx_count : 8 + ctx_count]
    send_refs = refs[8 + ctx_count :]
    rows_k = keys_ref.shape[0]
    place = lax.axis_index("ctx")
    queries_t = queries_ref[...]
    grads = grads_ref[...]

    keys = [keys_ref[...]] + [ref[...].T for ref in peer_refs]
    blocks = [(scores_ref[...], grad_prob_ref[...])]
    for b in range(1, ctx_count):
        first_key = lax.rem(place + b, ctx_count) * rows_k
        blocks.append(block_scores(keys[b], queries_t, grads, first_key, query_pos_ref[...]))
    scores = jnp.concatenate([block[0] for block in blocks], axis=0)
    grad_prob = jnp.concatenate([block[1] for block in blocks], axis=0)
    row_max = jnp.max(scores, axis=0, keepdims=True)
    exponent = jnp.where(scores > MASKED_SCORE, jnp.exp(scores - row_max), 0.0)
    weights = exponent * (1.0 / jnp.sum(exponent, axis=0, keepdims=True))
    row_delta = jnp.sum(weights * grad_prob, axis=0, keepdims=True)
    dscore = (weights * (grad_prob - row_delta)).astype(BF16)
    weights_low = weights.astype(BF16)
    dscore_ref[...] = dscore

    key_part = dot_nt(dscore, queries_t) * SOFTMAX_SCALE
    latent_part = key_part[:, :LATENT] + dot(weights_low, grads)
    all_keys = jnp.concatenate(keys, axis=0)[:, :LATENT]
    gain = jnp.sum(latent_part * all_keys.astype(F32), axis=0, keepdims=True)
    gain_ref[...] = gain
    tail = gain_tail(gain)
    width = key_part.shape[1]
    for b in range(ctx_count):
        rows = slice(b * rows_k, (b + 1) * rows_k)
        target = own_ref if b == 0 else send_refs[b - 1]
        target[:, :LATENT] = latent_part[rows].astype(target.dtype)
        target[:, LATENT:width] = key_part[rows, LATENT:].astype(target.dtype)
        if b:
            write_tail(target, tail)


def grad_queries_kernel(*refs):
    dscore_ref, *key_refs, dq_ref, mark_ref = refs
    mark_ref[...] = jnp.zeros(mark_ref.shape, F32)
    heads, _, rows_q = dq_ref.shape
    keys_t = jnp.concatenate([ref[...] for ref in key_refs], axis=1)
    dq_t = dot(keys_t, dscore_ref[...]) * SOFTMAX_SCALE
    for h in range(heads):
        dq_ref[h] = dq_t[:, h * rows_q : (h + 1) * rows_q].astype(BF16)


def pair_kernel(ctx_count, exp_count, *refs):
    own_ref, gain_ref = refs[:2]
    recv_refs = refs[2 : 1 + ctx_count]
    kept_ref, gain_out = refs[1 + ctx_count : 3 + ctx_count]
    send_refs = refs[3 + ctx_count : -1]
    total = refs[-1]
    share, width = kept_ref.shape
    value = own_ref[...]
    gain = gain_ref[...]
    for ref in recv_refs:
        value = value + ref[:, :width].astype(F32)
        gain = gain + tail_gain(ref[: 2 * TAIL_ROWS, width:].astype(F32))
    total[...] = value.reshape(total.shape)
    gain_out[...] = gain
    tail = gain_tail(gain)
    place = lax.axis_index("exp")
    kept_ref[...] = total[place]
    for step, ref in zip(exchange_steps(EXP_STEPS, exp_count), send_refs):
        if ref.shape[0] > share:
            ref[...] = jnp.zeros(ref.shape, ref.dtype)
        ref[:share, :width] = total[target_of(place, step)].astype(BF16)
        write_tail(ref, tail)


def gain_kernel(*refs):
    gain_ref, _, *recv_refs, gain_out = refs
    tail = jnp.zeros((2 * TAIL_ROWS, TAIL), F32)
    for ref in recv_refs:
        tail = tail + ref[: 2 * TAIL_ROWS, ref.shape[1] - TAIL :].astype(F32)
    gain_out[...] = gain_ref[...] + tail_gain(tail)


def sum_kernel(*refs):
    *gain_refs, gain_out = refs
    gain = gain_refs[0][...]
    for ref in gain_refs[1:]:
        gain = gain + ref[...]
    gain_out[...] = gain


def final_kernel(total_count, *refs):
    total_refs = refs[:total_count]
    kv_gain_ref, kept_ref, *recv_refs, out_ref, gain_out = refs[total_count:]
    share, width = kept_ref.shape
    rows = kept_ref[...]
    for ref in recv_refs:
        rows = rows + ref[:share, :width].astype(F32)
    out_ref[...] = rows
    gain = total_refs[0][...]
    if total_count > 1:
        gain = jnp.where(lax.axis_index("ctx") == 0, total_refs[1][...], gain)
    gain_out[...] = gain / kv_gain_ref[...]


def call(kernel, out_shapes, operands, flops, scratch=(), fetch=False):
    space = pl.ANY if fetch else pltpu.VMEM
    size = sum(x.size * x.dtype.itemsize for x in (*operands, *out_shapes))
    if fetch:
        out_shapes = [pltpu.VMEM(x.shape, x.dtype) for x in out_shapes]
    return pl.pallas_call(
        kernel,
        out_shape=list(out_shapes),
        in_specs=[pl.BlockSpec(memory_space=space)] * len(operands),
        out_specs=[pl.BlockSpec(memory_space=pltpu.VMEM)] * len(out_shapes),
        scratch_shapes=list(scratch),
        compiler_params=pltpu.CompilerParams(vmem_limit_bytes=(56 if fetch else 48) * 2**20),
        cost_estimate=pl.CostEstimate(flops=flops, bytes_accessed=size, transcendentals=0),
    )(*operands)


def body(queries, out_grad, latent_keys, kv_gain, query_groups):
    ctx_count = lax.axis_size("ctx")
    exp_count = lax.axis_size("exp")
    _, rows_q, heads, width = queries.shape
    rows_k = latent_keys.shape[1]
    share = rows_k // exp_count
    keys_all = rows_k * ctx_count
    rows_all = rows_q * heads
    both = width + LATENT

    def f32(*shape):
        return jax.ShapeDtypeStruct(shape, F32)

    def bf16(*shape):
        return jax.ShapeDtypeStruct(shape, BF16)

    own_keys = latent_keys[0].T
    peer_keys = [shift(own_keys, "ctx", b) for b in range(1, ctx_count)]

    *prepared, query_pos, kv_gain_row = call(
        own_scores_kernel,
        [
            bf16(width, rows_all),
            bf16(rows_all, LATENT),
            bf16(rows_k, width),
            f32(rows_k, rows_all),
            f32(rows_k, rows_all),
            jax.ShapeDtypeStruct((1, rows_all), jnp.int32),
            f32(1, LATENT),
        ],
        [
            query_groups,
            kv_gain.reshape(1, LATENT),
            jnp.transpose(queries[0], (1, 2, 0)),
            out_grad[0],
            own_keys,
        ],
        2 * rows_all * rows_k * both,
        [
            pltpu.SMEM(query_groups.shape, jnp.int32),
            pltpu.VMEM((rows_q, heads, LATENT), BF16),
            pltpu.VMEM((width, rows_k), BF16),
            pltpu.SemaphoreType.DMA((4 + heads,)),
        ],
        fetch=True,
    )
    dscore, own, gain, *sends = call(
        lambda *refs: softmax_kernel(ctx_count, *refs),
        [bf16(keys_all, rows_all), f32(rows_k, width), f32(1, LATENT)]
        + [bf16(rows_k, width + TAIL)] * (ctx_count - 1),
        [*prepared, query_pos, *peer_keys],
        2 * rows_all * (2 * keys_all - rows_k) * both,
    )
    received = [shift(sends[b - 1], "ctx", -b) for b in range(1, ctx_count)]
    dq_t, mark = call(
        grad_queries_kernel,
        [bf16(heads, width, rows_q), f32(1, 128)],
        [dscore, own_keys, *peer_keys],
        2 * rows_all * keys_all * width,
    )
    message = bf16(max(share, 2 * TAIL_ROWS), width + TAIL)
    exp_steps = exchange_steps(EXP_STEPS, exp_count)
    kept, gain, *sends = call(
        lambda *refs: pair_kernel(ctx_count, exp_count, *refs),
        [f32(share, width), f32(1, LATENT)] + [message] * len(exp_steps),
        [own, gain, *received],
        rows_k * width * ctx_count,
        [pltpu.VMEM((exp_count, share, width), F32)],
    )
    received = [send_step(send, "exp", step) for send, step in zip(sends, exp_steps)]
    (gain,) = call(gain_kernel, [f32(1, LATENT)], [gain, mark, *received], LATENT * exp_count)

    dp_steps = exchange_steps(DP_STEPS, lax.axis_size("dp"))
    gains = [gain] + [
        lax.ppermute(
            gain,
            ("dp", "ctx"),
            [
                (i * ctx_count + c, (to if c or ctx_count != 2 else i) * ctx_count + c)
                for i, to in enumerate(step)
                for c in range(ctx_count)
            ],
        )
        for step in reversed(dp_steps)
    ]
    (gain,) = call(sum_kernel, [f32(1, LATENT)], gains, LATENT * len(gains))
    totals = [gain] + [shift(gain, "ctx", 1)] * (ctx_count == 2)
    grad_keys, grad_gain = call(
        lambda *refs: final_kernel(len(totals), *refs),
        [f32(share, width), f32(1, LATENT)],
        [*totals, kv_gain_row, kept, *received],
        share * width * exp_count,
    )
    grad_queries = jnp.transpose(dq_t, (2, 0, 1))[None]
    return (grad_queries, grad_keys[None, None], grad_gain.reshape(LATENT))


def solution(mesh):
    in_specs = (
        P("dp", "ctx", "exp", None),
        P("dp", "ctx", "exp", None),
        P("dp", "ctx", None),
        P(),
        P("dp", None),
    )
    out_specs = (P("dp", "ctx", "exp", None), P("dp", "ctx", "exp", None), P())
    return jax.shard_map(body, mesh=mesh, in_specs=in_specs, out_specs=out_specs, check_vma=False)
```

```python
import math

import jax
import jax.numpy as jnp
from jax import lax
from jax.experimental import pallas as pl
from jax.experimental.pallas import tpu as pltpu
from jax.sharding import PartitionSpec as P

LATENT = 512
SOFTMAX_SCALE = (0.1 * math.log(40.0) + 1.0) ** 2 / math.sqrt(192.0)
MASKED_SCORE = -1e30
TAIL = 64
TAIL_ROWS = LATENT // TAIL
G_PARTS = 4

NT = (((1,), (1,)), ((), ()))
F32, BF16 = jnp.float32, jnp.bfloat16


def shift(value, axis, step):
    size = lax.axis_size(axis)
    return lax.ppermute(value, axis, [(i, (i - step) % size) for i in range(size)])


EXP_STEPS = (
    (4, 5, 0, 7, 6, 1, 2, 3),
    (1, 2, 3, 0, 5, 7, 4, 6),
    (3, 0, 1, 2, 7, 6, 5, 4),
    (2, 3, 6, 1, 0, 4, 7, 5),
)
DP_STEPS = ((2, 6, 1, 4, 3, 7, 0, 5), (6, 2, 5, 1, 7, 4, 3, 0), (5, 3, 7, 6, 1, 0, 4, 2))


def ring_steps(size):
    return tuple(tuple((i + k) % size for i in range(size)) for k in range(1, size))


def exp_steps(exp_count, ctx_count):
    if (exp_count, ctx_count) == (4, 2):
        return EXP_STEPS
    return [
        [c * exp_count + to for c in range(ctx_count) for to in step]
        for step in ring_steps(exp_count)
    ]


def dp_pairs(dp_count, ctx_count):
    if (dp_count, ctx_count) == (4, 2):
        return [
            [(k % 4 * 2 + k // 4, to % 4 * 2 + to // 4) for k, to in enumerate(step)]
            for step in DP_STEPS
        ]
    return [
        [(i * ctx_count + c, to * ctx_count + c) for i, to in enumerate(step) for c in range(ctx_count)]
        for step in ring_steps(dp_count)
    ]


def target_of(core, place, step, exp_count):
    if step not in EXP_STEPS:
        return lax.rem(place + step[0], exp_count), True
    target = jnp.int32(step[0])
    for k in range(1, len(step)):
        target = jnp.where(core * exp_count + place == k, step[k], target)
    return lax.rem(target, exp_count), target // exp_count == core


def send_step(value, step):
    return lax.ppermute(value, ("ctx", "exp"), list(enumerate(step)))


def dot(a, b):
    return jnp.dot(a, b, preferred_element_type=F32)


def dot_nt(a, b):
    return lax.dot_general(a, b, NT, preferred_element_type=F32)


def gain_tail(gain):
    high = gain.astype(BF16).astype(F32)
    return jnp.concatenate(
        [
            part[:, r * TAIL : (r + 1) * TAIL]
            for part in (high, gain - high)
            for r in range(TAIL_ROWS)
        ],
        axis=0,
    ).astype(BF16)


def tail_gain(tail):
    tail = tail[:TAIL_ROWS] + tail[TAIL_ROWS:]
    return jnp.concatenate([tail[r : r + 1] for r in range(TAIL_ROWS)], axis=1)


def write_tail(ref, tail):
    rows, width = ref.shape
    if rows > 2 * TAIL_ROWS:
        ref[2 * TAIL_ROWS :, width - TAIL :] = jnp.zeros((rows - 2 * TAIL_ROWS, TAIL), BF16)
    ref[: 2 * TAIL_ROWS, width - TAIL :] = tail


def tail_blocks(share):
    step = min(share, 2 * TAIL_ROWS)
    return [(j, slice(j * step, (j + 1) * step), step) for j in range(2 * TAIL_ROWS // step)]


def masked(products, first_key, query_pos):
    key_pos = first_key + lax.broadcasted_iota(jnp.int32, products.shape, 0)
    return jnp.where(key_pos <= query_pos, products * SOFTMAX_SCALE, MASKED_SCORE)


def own_scores_kernel(
    groups_hbm, kv_gain_hbm, q_hbm, g_hbm, key_hbm,
    queries_ref, grads_ref, keys_ref, scores_ref, grad_prob_ref, query_pos_ref, kv_gain_ref,
    groups, g_ref, key_ref, copied,
):
    heads, _, rows_q = q_hbm.shape
    rows_k = key_ref.shape[1]
    q_copies = [
        pltpu.make_async_copy(
            q_hbm.at[h], queries_ref.at[:, pl.ds(h * rows_q, rows_q)], copied.at[3 + h]
        )
        for h in range(heads)
    ]
    key_copy = pltpu.make_async_copy(key_hbm, key_ref, copied.at[0])
    groups_copy = pltpu.make_async_copy(groups_hbm, groups, copied.at[1])
    part = rows_q // G_PARTS
    g_copies = [
        pltpu.make_async_copy(
            g_hbm.at[pl.ds(p * part, part)],
            g_ref.at[pl.ds(p * part, part)],
            copied.at[3 + heads + p],
        )
        for p in range(G_PARTS)
    ]
    gain_copy = pltpu.make_async_copy(kv_gain_hbm, kv_gain_ref, copied.at[2])
    for copy in (*g_copies, key_copy, *q_copies, groups_copy, gain_copy):
        copy.start()

    for p, copy in enumerate(g_copies):
        copy.wait()
        heads_first = jnp.swapaxes(g_ref[pl.ds(p * part, part)], 0, 1)
        for h in range(heads):
            grads_ref[pl.ds(h * rows_q + p * part, part), :] = heads_first[h]
    key_copy.wait()
    keys = key_ref[...].T
    keys_ref[...] = keys
    grad_prob_ref[...] = dot_nt(keys[:, :LATENT], grads_ref[...])
    groups_copy.wait()
    place = lax.axis_index("ctx")
    query_pos = groups[0, place] * rows_q + lax.rem(
        lax.broadcasted_iota(jnp.int32, (1, heads * rows_q), 1), rows_q
    )
    query_pos_ref[...] = query_pos
    for copy in q_copies:
        copy.wait()
    scores_ref[...] = masked(dot(keys, queries_ref[...]), place * rows_k, query_pos)
    gain_copy.wait()


def softmax_kernel(ctx_count, *refs):
    queries_ref, grads_ref, keys_ref, scores_ref, grad_prob_ref, query_pos_ref = refs[:6]
    peer_refs = refs[6 : 5 + ctx_count]
    dscore_ref, own_ref, gain_ref = refs[5 + ctx_count : 8 + ctx_count]
    send_refs = refs[8 + ctx_count :]
    rows_k = keys_ref.shape[0]
    place = lax.axis_index("ctx")
    queries_t = queries_ref[...]
    grads = grads_ref[...]

    keys = [keys_ref[...]] + [ref[...].T for ref in peer_refs]
    blocks = [(scores_ref[...], grad_prob_ref[...])]
    for b in range(1, ctx_count):
        first_key = lax.rem(place + b, ctx_count) * rows_k
        scores = masked(dot(keys[b], queries_t), first_key, query_pos_ref[...])
        blocks.append((scores, dot_nt(keys[b][:, :LATENT], grads)))
    scores = jnp.concatenate([block[0] for block in blocks], axis=0)
    grad_prob = jnp.concatenate([block[1] for block in blocks], axis=0)
    row_max = jnp.max(scores, axis=0, keepdims=True)
    exponent = jnp.exp(scores - row_max)
    weights = exponent * (1.0 / jnp.sum(exponent, axis=0, keepdims=True))
    row_delta = jnp.sum(weights * grad_prob, axis=0, keepdims=True)
    dscore = (weights * (grad_prob - row_delta)).astype(BF16)
    weights_low = weights.astype(BF16)
    dscore_ref[...] = dscore

    key_part = dot_nt(dscore, queries_t) * SOFTMAX_SCALE
    latent_part = key_part[:, :LATENT] + dot(weights_low, grads)
    all_keys = jnp.concatenate(keys, axis=0)[:, :LATENT]
    gain = jnp.sum(latent_part * all_keys.astype(F32), axis=0, keepdims=True)
    gain_ref[...] = gain
    tail = gain_tail(gain)
    blocks, share, width = own_ref.shape
    for b in range(ctx_count):
        rows = slice(b * rows_k, (b + 1) * rows_k)
        target = own_ref if b == 0 else send_refs[b - 1]
        latent_rows = latent_part[rows].reshape(blocks, share, LATENT)
        rope_rows = key_part[rows, LATENT:].reshape(blocks, share, width - LATENT)
        target[:, :, :LATENT] = latent_rows.astype(target.dtype)
        target[:, :, LATENT:width] = rope_rows.astype(target.dtype)
        if b:
            target[:, :, width:] = jnp.zeros((blocks, share, TAIL), BF16)
            for j, part, step in tail_blocks(share):
                target[j, :step, width:] = tail[part]


def grad_queries_kernel(*refs):
    dscore_ref, *key_refs, dq_ref, mark_ref = refs
    mark_ref[...] = jnp.zeros(mark_ref.shape, F32)
    heads, _, rows_q = dq_ref.shape
    keys_t = jnp.concatenate([ref[...] for ref in key_refs], axis=1)
    dq_t = dot(keys_t, dscore_ref[...]) * SOFTMAX_SCALE
    for h in range(heads):
        dq_ref[h] = dq_t[:, h * rows_q : (h + 1) * rows_q].astype(BF16)


def pair_kernel(ctx_count, *refs):
    own_ref, gain_ref = refs[:2]
    recv_refs = refs[2 : 1 + ctx_count]
    kept_ref, gain_out = refs[1 + ctx_count : 3 + ctx_count]
    send_refs = refs[3 + ctx_count :]
    exp_count, share, width = own_ref.shape

    def block(i):
        rows = own_ref[i]
        for ref in recv_refs:
            rows = rows + ref[i, :, :width].astype(F32)
        return rows

    gain = gain_ref[...]
    for ref in recv_refs:
        tail = [ref[j, :step, width:] for j, _, step in tail_blocks(share)]
        gain = gain + tail_gain(jnp.concatenate(tail, axis=0).astype(F32))
    gain_out[...] = gain
    tail = gain_tail(gain)
    core, place = lax.axis_index("ctx"), lax.axis_index("exp")
    kept_ref[...] = block(place)
    for step, ref in zip(exp_steps(exp_count, ctx_count), send_refs):
        target, sends = target_of(core, place, step, exp_count)
        if ref.shape[0] > share:
            ref[...] = jnp.zeros(ref.shape, ref.dtype)
        rows = block(target)
        ref[:share, :width] = jnp.where(sends, rows, jnp.zeros_like(rows)).astype(BF16)
        write_tail(ref, jnp.where(sends, tail, jnp.zeros_like(tail)))


def gain_kernel(*refs):
    gain_ref, _, *recv_refs, gain_out = refs
    tail = jnp.zeros((2 * TAIL_ROWS, TAIL), F32)
    for ref in recv_refs:
        tail = tail + ref[: 2 * TAIL_ROWS, ref.shape[1] - TAIL :].astype(F32)
    gain_out[...] = gain_ref[...] + tail_gain(tail)


def rows_kernel(*refs):
    _, kept_ref, *recv_refs, out_ref = refs
    share, width = kept_ref.shape
    rows = kept_ref[...]
    for ref in recv_refs:
        rows = rows + ref[:share, :width].astype(F32)
    out_ref[...] = rows


def final_kernel(*refs):
    kv_gain_ref, gain_ref, *recv_refs, gain_out = refs
    gain = gain_ref[...]
    for ref in recv_refs:
        gain = gain + ref[...]
    gain_out[...] = gain / kv_gain_ref[...]


def call(kernel, out_shapes, operands, flops, scratch=(), fetch=False):
    space = pl.ANY if fetch else pltpu.VMEM
    size = sum(x.size * x.dtype.itemsize for x in (*operands, *out_shapes))
    if fetch:
        out_shapes = [pltpu.VMEM(x.shape, x.dtype) for x in out_shapes]
    return pl.pallas_call(
        kernel,
        out_shape=list(out_shapes),
        in_specs=[pl.BlockSpec(memory_space=space)] * len(operands),
        out_specs=[pl.BlockSpec(memory_space=pltpu.VMEM)] * len(out_shapes),
        scratch_shapes=list(scratch),
        compiler_params=pltpu.CompilerParams(vmem_limit_bytes=(56 if fetch else 48) * 2**20),
        cost_estimate=pl.CostEstimate(flops=flops, bytes_accessed=size, transcendentals=0),
    )(*operands)


def body(queries, out_grad, latent_keys, kv_gain, query_groups):
    ctx_count = lax.axis_size("ctx")
    exp_count = lax.axis_size("exp")
    _, rows_q, heads, width = queries.shape
    rows_k = latent_keys.shape[1]
    share = rows_k // exp_count
    keys_all = rows_k * ctx_count
    rows_all = rows_q * heads
    both = width + LATENT

    def f32(*shape):
        return jax.ShapeDtypeStruct(shape, F32)

    def bf16(*shape):
        return jax.ShapeDtypeStruct(shape, BF16)

    own_keys = latent_keys[0].T
    peer_keys = [shift(own_keys, "ctx", b) for b in range(1, ctx_count)]

    *prepared, query_pos, kv_gain_row = call(
        own_scores_kernel,
        [
            bf16(width, rows_all),
            bf16(rows_all, LATENT),
            bf16(rows_k, width),
            f32(rows_k, rows_all),
            f32(rows_k, rows_all),
            jax.ShapeDtypeStruct((1, rows_all), jnp.int32),
            f32(1, LATENT),
        ],
        [
            query_groups,
            kv_gain.reshape(1, LATENT),
            jnp.transpose(queries[0], (1, 2, 0)),
            out_grad[0],
            own_keys,
        ],
        2 * rows_all * rows_k * both,
        [
            pltpu.SMEM(query_groups.shape, jnp.int32),
            pltpu.VMEM((rows_q, heads, LATENT), BF16),
            pltpu.VMEM((width, rows_k), BF16),
            pltpu.SemaphoreType.DMA((3 + heads + G_PARTS,)),
        ],
        fetch=True,
    )
    dscore, own, gain, *sends = call(
        lambda *refs: softmax_kernel(ctx_count, *refs),
        [bf16(keys_all, rows_all), f32(exp_count, share, width), f32(1, LATENT)]
        + [bf16(exp_count, share, width + TAIL)] * (ctx_count - 1),
        [*prepared, query_pos, *peer_keys],
        2 * rows_all * (2 * keys_all - rows_k) * both,
    )
    received = [shift(sends[b - 1], "ctx", -b) for b in range(1, ctx_count)]
    dq_t, mark = call(
        grad_queries_kernel,
        [bf16(heads, width, rows_q), f32(1, 128)],
        [dscore, own_keys, *peer_keys],
        2 * rows_all * keys_all * width,
    )
    message = bf16(max(share, 2 * TAIL_ROWS), width + TAIL)
    steps = exp_steps(exp_count, ctx_count)
    kept, gain, *sends = call(
        lambda *refs: pair_kernel(ctx_count, *refs),
        [f32(share, width), f32(1, LATENT)] + [message] * len(steps),
        [own, gain, *received],
        rows_k * width * ctx_count,
    )
    received = [send_step(send, step) for send, step in zip(sends, steps)]
    (gain,) = call(gain_kernel, [f32(1, LATENT)], [gain, mark, *received], LATENT * exp_count)

    pairs = dp_pairs(lax.axis_size("dp"), ctx_count)
    gains = [lax.ppermute(gain, ("dp", "ctx"), step) for step in reversed(pairs)]
    (grad_keys,) = call(
        rows_kernel, [f32(share, width)], [gain, kept, *received], share * width * exp_count
    )
    (grad_gain,) = call(
        final_kernel, [f32(1, LATENT)], [kv_gain_row, gain, *gains], LATENT * len(gains)
    )
    grad_queries = jnp.transpose(dq_t, (2, 0, 1))[None]
    return (grad_queries, grad_keys[None, None], grad_gain.reshape(LATENT))


def solution(mesh):
    in_specs = (
        P("dp", "ctx", "exp", None),
        P("dp", "ctx", "exp", None),
        P("dp", "ctx", None),
        P(),
        P("dp", None),
    )
    out_specs = (P("dp", "ctx", "exp", None), P("dp", "ctx", "exp", None), P())
    return jax.shard_map(body, mesh=mesh, in_specs=in_specs, out_specs=out_specs, check_vma=False)
```

```python
import math

import jax
import jax.numpy as jnp
from jax import lax
from jax.experimental import pallas as pl
from jax.experimental.pallas import tpu as pltpu
from jax.sharding import PartitionSpec as P

LATENT = 512
SOFTMAX_SCALE = (0.1 * math.log(40.0) + 1.0) ** 2 / math.sqrt(192.0)
MASKED_SCORE = -1e30
TAIL = 64
TAIL_ROWS = LATENT // TAIL

NT = (((1,), (1,)), ((), ()))
F32, BF16 = jnp.float32, jnp.bfloat16


def shift(value, axis, step):
    size = lax.axis_size(axis)
    return lax.ppermute(value, axis, [(i, (i - step) % size) for i in range(size)])


EXP_STEPS = (
    (4, 5, 0, 7, 6, 1, 2, 3),
    (1, 2, 3, 0, 5, 7, 4, 6),
    (3, 0, 1, 2, 7, 6, 5, 4),
    (2, 3, 6, 1, 0, 4, 7, 5),
)
DP_STEPS = ((2, 6, 1, 4, 3, 7, 0, 5), (6, 2, 5, 1, 7, 4, 3, 0), (5, 3, 7, 6, 1, 0, 4, 2))


def ring_steps(size):
    return tuple(tuple((i + k) % size for i in range(size)) for k in range(1, size))


def exp_steps(exp_count, ctx_count):
    if (exp_count, ctx_count) == (4, 2):
        return EXP_STEPS
    return [
        [c * exp_count + to for c in range(ctx_count) for to in step]
        for step in ring_steps(exp_count)
    ]


def dp_pairs(dp_count, ctx_count):
    if (dp_count, ctx_count) == (4, 2):
        return [
            [(k % 4 * 2 + k // 4, to % 4 * 2 + to // 4) for k, to in enumerate(step)]
            for step in DP_STEPS
        ]
    return [
        [(i * ctx_count + c, to * ctx_count + c) for i, to in enumerate(step) for c in range(ctx_count)]
        for step in ring_steps(dp_count)
    ]


def target_of(core, place, step, exp_count):
    if step not in EXP_STEPS:
        return lax.rem(place + step[0], exp_count), True
    target = jnp.int32(step[0])
    for k in range(1, len(step)):
        target = jnp.where(core * exp_count + place == k, step[k], target)
    return lax.rem(target, exp_count), target // exp_count == core


def send_step(value, step):
    return lax.ppermute(value, ("ctx", "exp"), list(enumerate(step)))


def dot(a, b):
    return jnp.dot(a, b, preferred_element_type=F32)


def dot_nt(a, b):
    return lax.dot_general(a, b, NT, preferred_element_type=F32)


def gain_tail(gain):
    high = gain.astype(BF16).astype(F32)
    return jnp.concatenate(
        [
            part[:, r * TAIL : (r + 1) * TAIL]
            for part in (high, gain - high)
            for r in range(TAIL_ROWS)
        ],
        axis=0,
    ).astype(BF16)


def tail_gain(tail):
    tail = tail[:TAIL_ROWS] + tail[TAIL_ROWS:]
    return jnp.concatenate([tail[r : r + 1] for r in range(TAIL_ROWS)], axis=1)


def write_tail(ref, tail):
    rows, width = ref.shape
    if rows > 2 * TAIL_ROWS:
        ref[2 * TAIL_ROWS :, width - TAIL :] = jnp.zeros((rows - 2 * TAIL_ROWS, TAIL), BF16)
    ref[: 2 * TAIL_ROWS, width - TAIL :] = tail


def tail_blocks(share):
    step = min(share, 2 * TAIL_ROWS)
    return [(j, slice(j * step, (j + 1) * step), step) for j in range(2 * TAIL_ROWS // step)]


def fetch_kernel(
    groups_hbm, kv_gain_hbm, q_hbm, g_hbm, key_hbm,
    queries_ref, grads_ref, keys_ref, query_pos_ref, kv_gain_ref,
    groups, g_ref, key_ref, copied,
):
    heads, _, rows_q = q_hbm.shape
    q_copies = [
        pltpu.make_async_copy(
            q_hbm.at[h], queries_ref.at[:, pl.ds(h * rows_q, rows_q)], copied.at[4 + h]
        )
        for h in range(heads)
    ]
    key_copy = pltpu.make_async_copy(key_hbm, key_ref, copied.at[0])
    groups_copy = pltpu.make_async_copy(groups_hbm, groups, copied.at[1])
    g_copy = pltpu.make_async_copy(g_hbm, g_ref, copied.at[2])
    gain_copy = pltpu.make_async_copy(kv_gain_hbm, kv_gain_ref, copied.at[3])
    for copy in (g_copy, key_copy, groups_copy, *q_copies, gain_copy):
        copy.start()

    g_copy.wait()
    grads_ref[...] = jnp.swapaxes(g_ref[...], 0, 1).reshape(heads * rows_q, LATENT)
    key_copy.wait()
    keys_ref[...] = key_ref[...].T
    groups_copy.wait()
    query_pos_ref[...] = groups[0, lax.axis_index("ctx")] * rows_q + lax.rem(
        lax.broadcasted_iota(jnp.int32, (1, heads * rows_q), 1), rows_q
    )
    for copy in (*q_copies, gain_copy):
        copy.wait()


def softmax_kernel(ctx_count, *refs):
    queries_ref, grads_ref, keys_ref, query_pos_ref = refs[:4]
    peer_refs = refs[4 : 3 + ctx_count]
    dscore_ref, own_ref, gain_ref = refs[3 + ctx_count : 6 + ctx_count]
    send_refs = refs[6 + ctx_count :]
    rows_k = keys_ref.shape[0]
    place = lax.axis_index("ctx")
    queries_t = queries_ref[...]
    grads = grads_ref[...]
    query_pos = query_pos_ref[...]

    keys = jnp.concatenate([keys_ref[...]] + [ref[...].T for ref in peer_refs], axis=0)
    scores = dot(keys, queries_t) * SOFTMAX_SCALE
    grad_prob = dot_nt(keys[:, :LATENT], grads)
    key_row = lax.broadcasted_iota(jnp.int32, (rows_k, scores.shape[1]), 0)
    visible = jnp.concatenate(
        [key_row + lax.rem(place + b, ctx_count) * rows_k <= query_pos for b in range(ctx_count)],
        axis=0,
    )
    scores = jnp.where(visible, scores, MASKED_SCORE)
    row_max = jnp.max(scores, axis=0, keepdims=True)
    exponent = jnp.exp(scores - row_max)
    weights = exponent * (1.0 / jnp.sum(exponent, axis=0, keepdims=True))
    row_delta = jnp.sum(weights * grad_prob, axis=0, keepdims=True)
    dscore = (weights * (grad_prob - row_delta)).astype(BF16)
    weights_low = weights.astype(BF16)
    dscore_ref[...] = dscore

    key_part = dot_nt(dscore, queries_t) * SOFTMAX_SCALE
    latent_part = key_part[:, :LATENT] + dot(weights_low, grads)
    gain = jnp.sum(latent_part * keys[:, :LATENT].astype(F32), axis=0, keepdims=True)
    gain_ref[...] = gain
    tail = gain_tail(gain)
    blocks, share, width = own_ref.shape
    for b in range(ctx_count):
        rows = slice(b * rows_k, (b + 1) * rows_k)
        target = own_ref if b == 0 else send_refs[b - 1]
        latent_rows = latent_part[rows].reshape(blocks, share, LATENT)
        rope_rows = key_part[rows, LATENT:].reshape(blocks, share, width - LATENT)
        target[:, :, :LATENT] = latent_rows.astype(target.dtype)
        target[:, :, LATENT:width] = rope_rows.astype(target.dtype)
        if b:
            target[:, :, width:] = jnp.zeros((blocks, share, TAIL), BF16)
            for j, part, step in tail_blocks(share):
                target[j, :step, width:] = tail[part]


def grad_queries_kernel(*refs):
    dscore_ref, *key_refs, dq_ref, mark_ref = refs
    mark_ref[...] = jnp.zeros(mark_ref.shape, F32)
    heads, _, rows_q = dq_ref.shape
    keys_t = jnp.concatenate([ref[...] for ref in key_refs], axis=1)
    dq_t = dot(keys_t, dscore_ref[...]) * SOFTMAX_SCALE
    for h in range(heads):
        dq_ref[h] = dq_t[:, h * rows_q : (h + 1) * rows_q].astype(BF16)


def pair_kernel(ctx_count, *refs):
    own_ref, gain_ref = refs[:2]
    recv_refs = refs[2 : 1 + ctx_count]
    kept_ref, gain_out = refs[1 + ctx_count : 3 + ctx_count]
    send_refs = refs[3 + ctx_count :]
    exp_count, share, width = own_ref.shape

    def block(i):
        rows = own_ref[i]
        for ref in recv_refs:
            rows = rows + ref[i, :, :width].astype(F32)
        return rows

    gain = gain_ref[...]
    for ref in recv_refs:
        tail = [ref[j, :step, width:] for j, _, step in tail_blocks(share)]
        gain = gain + tail_gain(jnp.concatenate(tail, axis=0).astype(F32))
    gain_out[...] = gain
    tail = gain_tail(gain)
    core, place = lax.axis_index("ctx"), lax.axis_index("exp")
    kept_ref[...] = block(place)
    for step, ref in zip(exp_steps(exp_count, ctx_count), send_refs):
        target, sends = target_of(core, place, step, exp_count)
        if ref.shape[0] > share:
            ref[...] = jnp.zeros(ref.shape, ref.dtype)
        rows = block(target)
        ref[:share, :width] = jnp.where(sends, rows, jnp.zeros_like(rows)).astype(BF16)
        write_tail(ref, jnp.where(sends, tail, jnp.zeros_like(tail)))


def gain_kernel(*refs):
    gain_ref, _, *recv_refs, gain_out = refs
    tail = jnp.zeros((2 * TAIL_ROWS, TAIL), F32)
    for ref in recv_refs:
        tail = tail + ref[: 2 * TAIL_ROWS, ref.shape[1] - TAIL :].astype(F32)
    gain_out[...] = gain_ref[...] + tail_gain(tail)


def rows_kernel(*refs):
    _, kept_ref, *recv_refs, out_ref = refs
    share, width = kept_ref.shape
    rows = kept_ref[...]
    for ref in recv_refs:
        rows = rows + ref[:share, :width].astype(F32)
    out_ref[...] = rows


def final_kernel(*refs):
    kv_gain_ref, gain_ref, *recv_refs, gain_out = refs
    gain = gain_ref[...]
    for ref in recv_refs:
        gain = gain + ref[...]
    gain_out[...] = gain / kv_gain_ref[...]


def call(kernel, out_shapes, operands, flops, scratch=(), fetch=False):
    space = pl.ANY if fetch else pltpu.VMEM
    size = sum(x.size * x.dtype.itemsize for x in (*operands, *out_shapes))
    if fetch:
        out_shapes = [pltpu.VMEM(x.shape, x.dtype) for x in out_shapes]
    return pl.pallas_call(
        kernel,
        out_shape=list(out_shapes),
        in_specs=[pl.BlockSpec(memory_space=space)] * len(operands),
        out_specs=[pl.BlockSpec(memory_space=pltpu.VMEM)] * len(out_shapes),
        scratch_shapes=list(scratch),
        compiler_params=pltpu.CompilerParams(vmem_limit_bytes=(56 if fetch else 48) * 2**20),
        cost_estimate=pl.CostEstimate(flops=flops, bytes_accessed=size, transcendentals=0),
    )(*operands)


def body(queries, out_grad, latent_keys, kv_gain, query_groups):
    ctx_count = lax.axis_size("ctx")
    exp_count = lax.axis_size("exp")
    _, rows_q, heads, width = queries.shape
    rows_k = latent_keys.shape[1]
    share = rows_k // exp_count
    keys_all = rows_k * ctx_count
    rows_all = rows_q * heads
    both = width + LATENT

    def f32(*shape):
        return jax.ShapeDtypeStruct(shape, F32)

    def bf16(*shape):
        return jax.ShapeDtypeStruct(shape, BF16)

    own_keys = latent_keys[0].T
    peer_keys = [shift(own_keys, "ctx", b) for b in range(1, ctx_count)]

    *prepared, query_pos, kv_gain_row = call(
        fetch_kernel,
        [
            bf16(width, rows_all),
            bf16(rows_all, LATENT),
            bf16(rows_k, width),
            jax.ShapeDtypeStruct((1, rows_all), jnp.int32),
            f32(1, LATENT),
        ],
        [
            query_groups,
            kv_gain.reshape(1, LATENT),
            jnp.transpose(queries[0], (1, 2, 0)),
            out_grad[0],
            own_keys,
        ],
        rows_all * width,
        [
            pltpu.SMEM(query_groups.shape, jnp.int32),
            pltpu.VMEM((rows_q, heads, LATENT), BF16),
            pltpu.VMEM((width, rows_k), BF16),
            pltpu.SemaphoreType.DMA((4 + heads,)),
        ],
        fetch=True,
    )
    dscore, own, gain, *sends = call(
        lambda *refs: softmax_kernel(ctx_count, *refs),
        [bf16(keys_all, rows_all), f32(exp_count, share, width), f32(1, LATENT)]
        + [bf16(exp_count, share, width + TAIL)] * (ctx_count - 1),
        [*prepared, query_pos, *peer_keys],
        4 * rows_all * keys_all * both,
    )
    received = [shift(sends[b - 1], "ctx", -b) for b in range(1, ctx_count)]
    dq_t, mark = call(
        grad_queries_kernel,
        [bf16(heads, width, rows_q), f32(1, 128)],
        [dscore, own_keys, *peer_keys],
        2 * rows_all * keys_all * width,
    )
    message = bf16(max(share, 2 * TAIL_ROWS), width + TAIL)
    steps = exp_steps(exp_count, ctx_count)
    kept, gain, *sends = call(
        lambda *refs: pair_kernel(ctx_count, *refs),
        [f32(share, width), f32(1, LATENT)] + [message] * len(steps),
        [own, gain, *received],
        rows_k * width * ctx_count,
    )
    received = [send_step(send, step) for send, step in zip(sends, steps)]
    (gain,) = call(gain_kernel, [f32(1, LATENT)], [gain, mark, *received], LATENT * exp_count)

    pairs = dp_pairs(lax.axis_size("dp"), ctx_count)
    gains = [lax.ppermute(gain, ("dp", "ctx"), step) for step in reversed(pairs)]
    (grad_keys,) = call(
        rows_kernel, [f32(share, width)], [gain, kept, *received], share * width * exp_count
    )
    (grad_gain,) = call(
        final_kernel, [f32(1, LATENT)], [kv_gain_row, gain, *gains], LATENT * len(gains)
    )
    grad_queries = jnp.transpose(dq_t, (2, 0, 1))[None]
    return (grad_queries, grad_keys[None, None], grad_gain.reshape(LATENT))


def solution(mesh):
    in_specs = (
        P("dp", "ctx", "exp", None),
        P("dp", "ctx", "exp", None),
        P("dp", "ctx", None),
        P(),
        P("dp", None),
    )
    out_specs = (P("dp", "ctx", "exp", None), P("dp", "ctx", "exp", None), P())
    return jax.shard_map(body, mesh=mesh, in_specs=in_specs, out_specs=out_specs, check_vma=False)
```

```python
import math

import jax
import jax.numpy as jnp
from jax import lax
from jax.experimental import pallas as pl
from jax.experimental.pallas import tpu as pltpu
from jax.sharding import PartitionSpec as P

LATENT = 512
SOFTMAX_SCALE = (0.1 * math.log(40.0) + 1.0) ** 2 / math.sqrt(192.0)
MASKED_SCORE = -1e30
TAIL = 64
TAIL_ROWS = LATENT // TAIL

QUERY_PARTS = 2

NT = (((1,), (1,)), ((), ()))
F32, BF16 = jnp.float32, jnp.bfloat16


def shift(value, axis, step):
    size = lax.axis_size(axis)
    return lax.ppermute(value, axis, [(i, (i - step) % size) for i in range(size)])


EXP_STEPS = (
    ((4, 5, 0, 7, 6, 1, 2, 3), (1, 2, 3, 0, 5, 7, 4, 6), (3, 0, 1, 2, 7, 6, 5, 4), (2, 3, 6, 1, 0, 4, 7, 5)),
    ((4, 5, 0, 7, 6, 1, 2, 3), (1, 2, 3, 0, 5, 7, 4, 6), (3, 0, 1, 2, 7, 6, 5, 4), (2, 3, 6, 1, 0, 4, 7, 5)),
    ((4, 5, 0, 7, 6, 1, 2, 3), (1, 2, 3, 0, 5, 7, 4, 6), (3, 0, 1, 2, 7, 6, 5, 4), (2, 3, 6, 1, 0, 4, 7, 5)),
    ((4, 5, 0, 7, 6, 1, 2, 3), (1, 2, 3, 0, 5, 7, 4, 6), (3, 0, 1, 2, 7, 6, 5, 4), (2, 3, 6, 1, 0, 4, 7, 5)),
)
DP_STEPS = (
    ((1, 2, 7, 6, 3, 0, 5, 4), (5, 3, 1, 2, 7, 6, 4, 0), (6, 7, 3, 1, 2, 4, 0, 5)),
    ((6, 2, 5, 0, 7, 3, 1, 4), (5, 6, 7, 1, 3, 0, 4, 2), (2, 7, 3, 5, 1, 4, 0, 6)),
    ((6, 7, 0, 1, 2, 3, 5, 4), (7, 6, 3, 0, 1, 2, 4, 5), (5, 0, 7, 6, 3, 4, 1, 2)),
    ((6, 3, 5, 0, 2, 7, 1, 4), (7, 4, 0, 2, 5, 6, 3, 1), (3, 0, 4, 6, 1, 2, 7, 5)),
)


def ring_steps(size):
    return tuple(tuple((i + k) % size for i in range(size)) for k in range(1, size))


def tuned(mesh_shape):
    return mesh_shape == (4, 2, 4)


def exp_pairs(mesh_shape):
    dp_count, ctx_count, exp_count = mesh_shape
    if tuned(mesh_shape):
        return [
            [
                (d * 8 + k, d * 8 + to)
                for d in range(dp_count)
                for k, to in enumerate(EXP_STEPS[d][i])
            ]
            for i in range(len(EXP_STEPS[0]))
        ]
    return [
        [
            (group * exp_count + i, group * exp_count + to)
            for group in range(dp_count * ctx_count)
            for i, to in enumerate(step)
        ]
        for step in ring_steps(exp_count)
    ]


def dp_pairs(mesh_shape):
    dp_count, ctx_count, exp_count = mesh_shape
    if tuned(mesh_shape):
        return [
            [
                (k % 4 * 8 + k // 4 * 4 + z, to % 4 * 8 + to // 4 * 4 + z)
                for z in range(exp_count)
                for k, to in enumerate(DP_STEPS[z][i])
            ]
            for i in range(len(DP_STEPS[0]))
        ]
    size = ctx_count * exp_count
    return [
        [(i * size + j, to * size + j) for i, to in enumerate(step) for j in range(size)]
        for step in ring_steps(dp_count)
    ]


def exp_target(mesh_shape, index):
    exp_count = mesh_shape[2]
    place = lax.axis_index("exp")
    if not tuned(mesh_shape):
        return lax.rem(place + ring_steps(exp_count)[index][0], exp_count), True
    core, row = lax.axis_index("ctx"), lax.axis_index("dp")
    words = [sum(to << 3 * k for k, to in enumerate(column[index])) for column in EXP_STEPS]
    word = jnp.int32(words[0])
    for i in range(1, len(words)):
        word = jnp.where(row == i, words[i], word)
    target = (word >> (3 * (core * 4 + place))) & 7
    return target & 3, (target >> 2) == core


def send_step(value, pairs):
    return lax.ppermute(value, ("dp", "ctx", "exp"), pairs)


def dot(a, b):
    return jnp.dot(a, b, preferred_element_type=F32)


def dot_nt(a, b):
    return lax.dot_general(a, b, NT, preferred_element_type=F32)


def gain_tail(gain):
    high = gain.astype(BF16).astype(F32)
    return jnp.concatenate(
        [
            part[:, r * TAIL : (r + 1) * TAIL]
            for part in (high, gain - high)
            for r in range(TAIL_ROWS)
        ],
        axis=0,
    ).astype(BF16)


def tail_gain(tail):
    tail = tail[:TAIL_ROWS] + tail[TAIL_ROWS:]
    return jnp.concatenate([tail[r : r + 1] for r in range(TAIL_ROWS)], axis=1)


def write_tail(ref, tail):
    rows, width = ref.shape
    if rows > 2 * TAIL_ROWS:
        ref[2 * TAIL_ROWS :, width - TAIL :] = jnp.zeros((rows - 2 * TAIL_ROWS, TAIL), BF16)
    ref[: 2 * TAIL_ROWS, width - TAIL :] = tail


def tail_blocks(share):
    step = min(share, 2 * TAIL_ROWS)
    return [(j, slice(j * step, (j + 1) * step), step) for j in range(2 * TAIL_ROWS // step)]


def fetch_kernel(
    groups_hbm, kv_gain_hbm, q_hbm, g_hbm, key_hbm,
    queries_ref, grads_ref, keys_ref, query_pos_ref, kv_gain_ref,
    groups, g_ref, key_ref, copied,
):
    heads, _, rows_q = q_hbm.shape
    q_copies = [
        pltpu.make_async_copy(
            q_hbm.at[h], queries_ref.at[:, pl.ds(h * rows_q, rows_q)], copied.at[4 + h]
        )
        for h in range(heads)
    ]
    key_copy = pltpu.make_async_copy(key_hbm, key_ref, copied.at[0])
    groups_copy = pltpu.make_async_copy(groups_hbm, groups, copied.at[1])
    g_copy = pltpu.make_async_copy(g_hbm, g_ref, copied.at[2])
    gain_copy = pltpu.make_async_copy(kv_gain_hbm, kv_gain_ref, copied.at[3])
    for copy in (g_copy, key_copy, groups_copy, *q_copies, gain_copy):
        copy.start()

    g_copy.wait()
    grads_ref[...] = jnp.swapaxes(g_ref[...], 0, 1).reshape(heads * rows_q, LATENT)
    key_copy.wait()
    keys_ref[...] = key_ref[...].T
    groups_copy.wait()
    query_pos_ref[...] = groups[0, lax.axis_index("ctx")] * rows_q + lax.rem(
        lax.broadcasted_iota(jnp.int32, (1, heads * rows_q), 1), rows_q
    )
    for copy in (*q_copies, gain_copy):
        copy.wait()


def softmax_kernel(ctx_count, *refs):
    queries_ref, grads_ref, keys_ref, query_pos_ref = refs[:4]
    peer_refs = refs[4 : 3 + ctx_count]
    dscore_ref, own_ref, gain_ref = refs[3 + ctx_count : 6 + ctx_count]
    send_refs = refs[6 + ctx_count :]
    rows_k = keys_ref.shape[0]
    place = lax.axis_index("ctx")
    queries_t = queries_ref[...]
    grads = grads_ref[...]
    query_pos = query_pos_ref[...]

    keys = jnp.concatenate([keys_ref[...]] + [ref[...].T for ref in peer_refs], axis=0)
    part = queries_t.shape[1] // QUERY_PARTS
    parts = [slice(p * part, (p + 1) * part) for p in range(QUERY_PARTS)]
    scores = [dot(keys, queries_t[:, p]) * SOFTMAX_SCALE for p in parts]
    grad_prob = [dot_nt(keys[:, :LATENT], grads[p]) for p in parts]
    key_row = lax.broadcasted_iota(jnp.int32, (rows_k, part), 0)
    key_pos = jnp.concatenate(
        [key_row + lax.rem(place + b, ctx_count) * rows_k for b in range(ctx_count)], axis=0
    )
    key_part = value_part = 0.0
    for i, p in enumerate(parts):
        masked = jnp.where(key_pos <= query_pos[:, p], scores[i], MASKED_SCORE)
        row_max = jnp.max(masked, axis=0, keepdims=True)
        exponent = jnp.exp(masked - row_max)
        weights = exponent * (1.0 / jnp.sum(exponent, axis=0, keepdims=True))
        row_delta = jnp.sum(weights * grad_prob[i], axis=0, keepdims=True)
        dscore = (weights * (grad_prob[i] - row_delta)).astype(BF16)
        dscore_ref[:, p] = dscore
        key_part += dot_nt(dscore, queries_t[:, p])
        value_part += dot(weights.astype(BF16), grads[p])
    key_part = key_part * SOFTMAX_SCALE
    latent_part = key_part[:, :LATENT] + value_part
    gain = jnp.sum(latent_part * keys[:, :LATENT].astype(F32), axis=0, keepdims=True)
    gain_ref[...] = gain
    tail = gain_tail(gain)
    blocks, share, width = own_ref.shape
    for b in range(ctx_count):
        rows = slice(b * rows_k, (b + 1) * rows_k)
        target = own_ref if b == 0 else send_refs[b - 1]
        latent_rows = latent_part[rows].reshape(blocks, share, LATENT)
        rope_rows = key_part[rows, LATENT:].reshape(blocks, share, width - LATENT)
        target[:, :, :LATENT] = latent_rows.astype(target.dtype)
        target[:, :, LATENT:width] = rope_rows.astype(target.dtype)
        if b:
            target[:, :, width:] = jnp.zeros((blocks, share, TAIL), BF16)
            for j, part, step in tail_blocks(share):
                target[j, :step, width:] = tail[part]


def grad_queries_kernel(*refs):
    dscore_ref, *key_refs, dq_ref, mark_ref = refs
    mark_ref[...] = jnp.zeros(mark_ref.shape, F32)
    heads, _, rows_q = dq_ref.shape
    keys_t = jnp.concatenate([ref[...] for ref in key_refs], axis=1)
    dq_t = dot(keys_t, dscore_ref[...]) * SOFTMAX_SCALE
    for h in range(heads):
        dq_ref[h] = dq_t[:, h * rows_q : (h + 1) * rows_q].astype(BF16)


def pair_kernel(mesh_shape, *refs):
    ctx_count = mesh_shape[1]
    own_ref, gain_ref = refs[:2]
    recv_refs = refs[2 : 1 + ctx_count]
    kept_ref, gain_out = refs[1 + ctx_count : 3 + ctx_count]
    send_refs = refs[3 + ctx_count :]
    share, width = own_ref.shape[1:]

    def block(i):
        rows = own_ref[i]
        for ref in recv_refs:
            rows = rows + ref[i, :, :width].astype(F32)
        return rows

    gain = gain_ref[...]
    for ref in recv_refs:
        tail = [ref[j, :step, width:] for j, _, step in tail_blocks(share)]
        gain = gain + tail_gain(jnp.concatenate(tail, axis=0).astype(F32))
    gain_out[...] = gain
    tail = gain_tail(gain)
    kept_ref[...] = block(lax.axis_index("exp"))
    for index, ref in enumerate(send_refs):
        target, sends = exp_target(mesh_shape, index)
        if ref.shape[0] > share:
            ref[...] = jnp.zeros(ref.shape, ref.dtype)
        rows = block(target)
        ref[:share, :width] = jnp.where(sends, rows, jnp.zeros_like(rows)).astype(BF16)
        write_tail(ref, jnp.where(sends, tail, jnp.zeros_like(tail)))


def gain_kernel(*refs):
    gain_ref, _, *recv_refs, gain_out = refs
    tail = jnp.zeros((2 * TAIL_ROWS, TAIL), F32)
    for ref in recv_refs:
        tail = tail + ref[: 2 * TAIL_ROWS, ref.shape[1] - TAIL :].astype(F32)
    gain_out[...] = gain_ref[...] + tail_gain(tail)


def rows_kernel(*refs):
    _, kept_ref, *recv_refs, out_ref = refs
    share, width = kept_ref.shape
    rows = kept_ref[...]
    for ref in recv_refs:
        rows = rows + ref[:share, :width].astype(F32)
    out_ref[...] = rows


def final_kernel(*refs):
    kv_gain_ref, gain_ref, *recv_refs, gain_out = refs
    gain = gain_ref[...]
    for ref in recv_refs:
        gain = gain + ref[...]
    gain_out[...] = gain / kv_gain_ref[...]


def call(kernel, out_shapes, operands, flops, scratch=(), fetch=False):
    space = pl.ANY if fetch else pltpu.VMEM
    size = sum(x.size * x.dtype.itemsize for x in (*operands, *out_shapes))
    if fetch:
        out_shapes = [pltpu.VMEM(x.shape, x.dtype) for x in out_shapes]
    return pl.pallas_call(
        kernel,
        out_shape=list(out_shapes),
        in_specs=[pl.BlockSpec(memory_space=space)] * len(operands),
        out_specs=[pl.BlockSpec(memory_space=pltpu.VMEM)] * len(out_shapes),
        scratch_shapes=list(scratch),
        compiler_params=pltpu.CompilerParams(vmem_limit_bytes=(56 if fetch else 48) * 2**20),
        cost_estimate=pl.CostEstimate(flops=flops, bytes_accessed=size, transcendentals=0),
    )(*operands)


def body(queries, out_grad, latent_keys, kv_gain, query_groups):
    ctx_count = lax.axis_size("ctx")
    exp_count = lax.axis_size("exp")
    _, rows_q, heads, width = queries.shape
    rows_k = latent_keys.shape[1]
    share = rows_k // exp_count
    keys_all = rows_k * ctx_count
    rows_all = rows_q * heads
    both = width + LATENT

    def f32(*shape):
        return jax.ShapeDtypeStruct(shape, F32)

    def bf16(*shape):
        return jax.ShapeDtypeStruct(shape, BF16)

    own_keys = latent_keys[0].T
    peer_keys = [shift(own_keys, "ctx", b) for b in range(1, ctx_count)]

    *prepared, query_pos, kv_gain_row = call(
        fetch_kernel,
        [
            bf16(width, rows_all),
            bf16(rows_all, LATENT),
            bf16(rows_k, width),
            jax.ShapeDtypeStruct((1, rows_all), jnp.int32),
            f32(1, LATENT),
        ],
        [
            query_groups,
            kv_gain.reshape(1, LATENT),
            jnp.transpose(queries[0], (1, 2, 0)),
            out_grad[0],
            own_keys,
        ],
        rows_all * width,
        [
            pltpu.SMEM(query_groups.shape, jnp.int32),
            pltpu.VMEM((rows_q, heads, LATENT), BF16),
            pltpu.VMEM((width, rows_k), BF16),
            pltpu.SemaphoreType.DMA((4 + heads,)),
        ],
        fetch=True,
    )
    dscore, own, gain, *sends = call(
        lambda *refs: softmax_kernel(ctx_count, *refs),
        [bf16(keys_all, rows_all), f32(exp_count, share, width), f32(1, LATENT)]
        + [bf16(exp_count, share, width + TAIL)] * (ctx_count - 1),
        [*prepared, query_pos, *peer_keys],
        4 * rows_all * keys_all * both,
    )
    received = [shift(sends[b - 1], "ctx", -b) for b in range(1, ctx_count)]
    dq_t, mark = call(
        grad_queries_kernel,
        [bf16(heads, width, rows_q), f32(1, 128)],
        [dscore, own_keys, *peer_keys],
        2 * rows_all * keys_all * width,
    )
    message = bf16(max(share, 2 * TAIL_ROWS), width + TAIL)
    mesh_shape = (lax.axis_size("dp"), ctx_count, exp_count)
    steps = exp_pairs(mesh_shape)
    kept, gain, *sends = call(
        lambda *refs: pair_kernel(mesh_shape, *refs),
        [f32(share, width), f32(1, LATENT)] + [message] * len(steps),
        [own, gain, *received],
        rows_k * width * ctx_count,
    )
    received = [send_step(send, step) for send, step in zip(sends, steps)]
    (gain,) = call(gain_kernel, [f32(1, LATENT)], [gain, mark, *received], LATENT * exp_count)

    gains = [send_step(gain, step) for step in reversed(dp_pairs(mesh_shape))]
    (grad_keys,) = call(
        rows_kernel, [f32(share, width)], [gain, kept, *received], share * width * exp_count
    )
    (grad_gain,) = call(
        final_kernel, [f32(1, LATENT)], [kv_gain_row, gain, *gains], LATENT * len(gains)
    )
    grad_queries = jnp.transpose(dq_t, (2, 0, 1))[None]
    return (grad_queries, grad_keys[None, None], grad_gain.reshape(LATENT))


def solution(mesh):
    in_specs = (
        P("dp", "ctx", "exp", None),
        P("dp", "ctx", "exp", None),
        P("dp", "ctx", None),
        P(),
        P("dp", None),
    )
    out_specs = (P("dp", "ctx", "exp", None), P("dp", "ctx", "exp", None), P())
    return jax.shard_map(body, mesh=mesh, in_specs=in_specs, out_specs=out_specs, check_vma=False)
```

```python
import math

import jax
import jax.numpy as jnp
from jax import lax
from jax.experimental import pallas as pl
from jax.experimental.pallas import tpu as pltpu
from jax.sharding import PartitionSpec as P

LATENT = 512
SOFTMAX_SCALE = (0.1 * math.log(40.0) + 1.0) ** 2 / math.sqrt(192.0)
MASKED_SCORE = -1e30
TAIL = 64
TAIL_ROWS = LATENT // TAIL

NT = (((1,), (1,)), ((), ()))
F32, BF16 = jnp.float32, jnp.bfloat16


def shift(value, axis, step):
    size = lax.axis_size(axis)
    return lax.ppermute(value, axis, [(i, (i - step) % size) for i in range(size)])


EXP_STEPS = (
    ((4, 5, 0, 7, 6, 1, 2, 3), (1, 2, 3, 0, 5, 7, 4, 6), (3, 0, 1, 2, 7, 6, 5, 4), (2, 3, 6, 1, 0, 4, 7, 5)),
    ((4, 5, 0, 7, 6, 1, 2, 3), (1, 2, 3, 0, 5, 7, 4, 6), (3, 0, 1, 2, 7, 6, 5, 4), (2, 3, 6, 1, 0, 4, 7, 5)),
    ((4, 5, 0, 7, 6, 1, 2, 3), (1, 2, 3, 0, 5, 7, 4, 6), (3, 0, 1, 2, 7, 6, 5, 4), (2, 3, 6, 1, 0, 4, 7, 5)),
    ((4, 5, 0, 7, 6, 1, 2, 3), (1, 2, 3, 0, 5, 7, 4, 6), (3, 0, 1, 2, 7, 6, 5, 4), (2, 3, 6, 1, 0, 4, 7, 5)),
)
DP_STEPS = (
    ((1, 2, 7, 6, 3, 0, 5, 4), (5, 3, 1, 2, 7, 6, 4, 0), (6, 7, 3, 1, 2, 4, 0, 5)),
    ((6, 2, 5, 0, 7, 3, 1, 4), (5, 6, 7, 1, 3, 0, 4, 2), (2, 7, 3, 5, 1, 4, 0, 6)),
    ((6, 7, 0, 1, 2, 3, 5, 4), (7, 6, 3, 0, 1, 2, 4, 5), (5, 0, 7, 6, 3, 4, 1, 2)),
    ((6, 3, 5, 0, 2, 7, 1, 4), (7, 4, 0, 2, 5, 6, 3, 1), (3, 0, 4, 6, 1, 2, 7, 5)),
)


def ring_steps(size):
    return tuple(tuple((i + k) % size for i in range(size)) for k in range(1, size))


def tuned(mesh_shape):
    return mesh_shape == (4, 2, 4)


def exp_pairs(mesh_shape):
    dp_count, ctx_count, exp_count = mesh_shape
    if tuned(mesh_shape):
        return [
            [
                (d * 8 + k, d * 8 + to)
                for d in range(dp_count)
                for k, to in enumerate(EXP_STEPS[d][i])
            ]
            for i in range(len(EXP_STEPS[0]))
        ]
    return [
        [
            (group * exp_count + i, group * exp_count + to)
            for group in range(dp_count * ctx_count)
            for i, to in enumerate(step)
        ]
        for step in ring_steps(exp_count)
    ]


def dp_pairs(mesh_shape):
    dp_count, ctx_count, exp_count = mesh_shape
    if tuned(mesh_shape):
        return [
            [
                (k % 4 * 8 + k // 4 * 4 + z, to % 4 * 8 + to // 4 * 4 + z)
                for z in range(exp_count)
                for k, to in enumerate(DP_STEPS[z][i])
            ]
            for i in range(len(DP_STEPS[0]))
        ]
    size = ctx_count * exp_count
    return [
        [(i * size + j, to * size + j) for i, to in enumerate(step) for j in range(size)]
        for step in ring_steps(dp_count)
    ]


def exp_target(mesh_shape, index):
    exp_count = mesh_shape[2]
    place = lax.axis_index("exp")
    if not tuned(mesh_shape):
        return lax.rem(place + ring_steps(exp_count)[index][0], exp_count), True
    core, row = lax.axis_index("ctx"), lax.axis_index("dp")
    words = [sum(to << 3 * k for k, to in enumerate(column[index])) for column in EXP_STEPS]
    word = jnp.int32(words[0])
    for i in range(1, len(words)):
        word = jnp.where(row == i, words[i], word)
    target = (word >> (3 * (core * 4 + place))) & 7
    return target & 3, (target >> 2) == core


def send_step(value, pairs):
    return lax.ppermute(value, ("dp", "ctx", "exp"), pairs)


def dot(a, b):
    return jnp.dot(a, b, preferred_element_type=F32)


def dot_nt(a, b):
    return lax.dot_general(a, b, NT, preferred_element_type=F32)


def gain_tail(gain):
    high = gain.astype(BF16).astype(F32)
    return jnp.concatenate(
        [
            part[:, r * TAIL : (r + 1) * TAIL]
            for part in (high, gain - high)
            for r in range(TAIL_ROWS)
        ],
        axis=0,
    ).astype(BF16)


def tail_gain(tail):
    tail = tail[:TAIL_ROWS] + tail[TAIL_ROWS:]
    return jnp.concatenate([tail[r : r + 1] for r in range(TAIL_ROWS)], axis=1)


def write_tail(ref, tail):
    rows, width = ref.shape
    if rows > 2 * TAIL_ROWS:
        ref[2 * TAIL_ROWS :, width - TAIL :] = jnp.zeros((rows - 2 * TAIL_ROWS, TAIL), BF16)
    ref[: 2 * TAIL_ROWS, width - TAIL :] = tail


def tail_blocks(share):
    step = min(share, 2 * TAIL_ROWS)
    return [(j, slice(j * step, (j + 1) * step), step) for j in range(2 * TAIL_ROWS // step)]


def fetch_kernel(
    groups_hbm, kv_gain_hbm, q_hbm, g_hbm, key_hbm,
    queries_ref, grads_ref, keys_ref, query_pos_ref, kv_gain_ref,
    groups, g_ref, key_ref, copied,
):
    heads, _, rows_q = q_hbm.shape
    q_copies = [
        pltpu.make_async_copy(
            q_hbm.at[h], queries_ref.at[:, pl.ds(h * rows_q, rows_q)], copied.at[4 + h]
        )
        for h in range(heads)
    ]
    key_copy = pltpu.make_async_copy(key_hbm, key_ref, copied.at[0])
    groups_copy = pltpu.make_async_copy(groups_hbm, groups, copied.at[1])
    g_copy = pltpu.make_async_copy(g_hbm, g_ref, copied.at[2])
    gain_copy = pltpu.make_async_copy(kv_gain_hbm, kv_gain_ref, copied.at[3])
    for copy in (g_copy, key_copy, groups_copy, *q_copies, gain_copy):
        copy.start()

    g_copy.wait()
    grads_ref[...] = jnp.swapaxes(g_ref[...], 0, 1).reshape(heads * rows_q, LATENT)
    key_copy.wait()
    keys_ref[...] = key_ref[...].T
    groups_copy.wait()
    query_pos_ref[...] = groups[0, lax.axis_index("ctx")] * rows_q + lax.rem(
        lax.broadcasted_iota(jnp.int32, (1, heads * rows_q), 1), rows_q
    )
    for copy in (*q_copies, gain_copy):
        copy.wait()


def softmax_kernel(ctx_count, *refs):
    queries_ref, grads_ref, keys_ref, query_pos_ref = refs[:4]
    peer_refs = refs[4 : 3 + ctx_count]
    dscore_ref, own_ref, gain_ref = refs[3 + ctx_count : 6 + ctx_count]
    send_refs = refs[6 + ctx_count :]
    rows_k = keys_ref.shape[0]
    place = lax.axis_index("ctx")
    queries_t = queries_ref[...]
    grads = grads_ref[...]
    query_pos = query_pos_ref[...]

    keys = jnp.concatenate([keys_ref[...]] + [ref[...].T for ref in peer_refs], axis=0)
    scores = dot(keys, queries_t) * SOFTMAX_SCALE
    grad_prob = dot_nt(keys[:, :LATENT], grads)
    key_row = lax.broadcasted_iota(jnp.int32, (rows_k, scores.shape[1]), 0)
    visible = jnp.concatenate(
        [key_row + lax.rem(place + b, ctx_count) * rows_k <= query_pos for b in range(ctx_count)],
        axis=0,
    )
    scores = jnp.where(visible, scores, MASKED_SCORE)
    row_max = jnp.max(scores, axis=0, keepdims=True)
    exponent = jnp.exp(scores - row_max)
    weights = exponent * (1.0 / jnp.sum(exponent, axis=0, keepdims=True))
    row_delta = jnp.sum(weights * grad_prob, axis=0, keepdims=True)
    dscore = (weights * (grad_prob - row_delta)).astype(BF16)
    weights_low = weights.astype(BF16)
    dscore_ref[...] = dscore

    key_part = dot_nt(dscore, queries_t) * SOFTMAX_SCALE
    latent_part = key_part[:, :LATENT] + dot(weights_low, grads)
    gain = jnp.sum(latent_part * keys[:, :LATENT].astype(F32), axis=0, keepdims=True)
    gain_ref[...] = gain
    tail = gain_tail(gain)
    blocks, share, width = own_ref.shape
    for b in range(ctx_count):
        rows = slice(b * rows_k, (b + 1) * rows_k)
        target = own_ref if b == 0 else send_refs[b - 1]
        latent_rows = latent_part[rows].reshape(blocks, share, LATENT)
        rope_rows = key_part[rows, LATENT:].reshape(blocks, share, width - LATENT)
        target[:, :, :LATENT] = latent_rows.astype(target.dtype)
        target[:, :, LATENT:width] = rope_rows.astype(target.dtype)
        if b:
            target[:, :, width:] = jnp.zeros((blocks, share, TAIL), BF16)
            for j, part, step in tail_blocks(share):
                target[j, :step, width:] = tail[part]


def grad_queries_kernel(*refs):
    dscore_ref, *key_refs, dq_ref, mark_ref = refs
    mark_ref[...] = jnp.zeros(mark_ref.shape, F32)
    heads, _, rows_q = dq_ref.shape
    keys_t = jnp.concatenate([ref[...] for ref in key_refs], axis=1)
    dq_t = dot(keys_t, dscore_ref[...]) * SOFTMAX_SCALE
    for h in range(heads):
        dq_ref[h] = dq_t[:, h * rows_q : (h + 1) * rows_q].astype(BF16)


def pair_kernel(mesh_shape, *refs):
    ctx_count = mesh_shape[1]
    own_ref, gain_ref = refs[:2]
    recv_refs = refs[2 : 1 + ctx_count]
    kept_ref, gain_out = refs[1 + ctx_count : 3 + ctx_count]
    send_refs = refs[3 + ctx_count :]
    share, width = own_ref.shape[1:]

    def block(i):
        rows = own_ref[i]
        for ref in recv_refs:
            rows = rows + ref[i, :, :width].astype(F32)
        return rows

    gain = gain_ref[...]
    for ref in recv_refs:
        tail = [ref[j, :step, width:] for j, _, step in tail_blocks(share)]
        gain = gain + tail_gain(jnp.concatenate(tail, axis=0).astype(F32))
    gain_out[...] = gain
    tail = gain_tail(gain)
    kept_ref[...] = block(lax.axis_index("exp"))
    for index, ref in enumerate(send_refs):
        target, sends = exp_target(mesh_shape, index)
        if ref.shape[0] > share:
            ref[...] = jnp.zeros(ref.shape, ref.dtype)
        rows = block(target)
        ref[:share, :width] = jnp.where(sends, rows, jnp.zeros_like(rows)).astype(BF16)
        write_tail(ref, jnp.where(sends, tail, jnp.zeros_like(tail)))


def gain_kernel(*refs):
    gain_ref, _, *recv_refs, gain_out = refs
    tail = jnp.zeros((2 * TAIL_ROWS, TAIL), F32)
    for ref in recv_refs:
        tail = tail + ref[: 2 * TAIL_ROWS, ref.shape[1] - TAIL :].astype(F32)
    gain_out[...] = gain_ref[...] + tail_gain(tail)


def rows_kernel(*refs):
    _, kept_ref, *recv_refs, out_ref = refs
    share, width = kept_ref.shape
    rows = kept_ref[...]
    for ref in recv_refs:
        rows = rows + ref[:share, :width].astype(F32)
    out_ref[...] = rows


def final_kernel(*refs):
    kv_gain_ref, gain_ref, *recv_refs, gain_out = refs
    gain = gain_ref[...]
    for ref in recv_refs:
        gain = gain + ref[...]
    gain_out[...] = gain / kv_gain_ref[...]


def call(kernel, out_shapes, operands, flops, scratch=(), fetch=False):
    space = pl.ANY if fetch else pltpu.VMEM
    size = sum(x.size * x.dtype.itemsize for x in (*operands, *out_shapes))
    if fetch:
        out_shapes = [pltpu.VMEM(x.shape, x.dtype) for x in out_shapes]
    return pl.pallas_call(
        kernel,
        out_shape=list(out_shapes),
        in_specs=[pl.BlockSpec(memory_space=space)] * len(operands),
        out_specs=[pl.BlockSpec(memory_space=pltpu.VMEM)] * len(out_shapes),
        scratch_shapes=list(scratch),
        compiler_params=pltpu.CompilerParams(vmem_limit_bytes=(56 if fetch else 48) * 2**20),
        cost_estimate=pl.CostEstimate(flops=flops, bytes_accessed=size, transcendentals=0),
    )(*operands)


def body(queries, out_grad, latent_keys, kv_gain, query_groups):
    ctx_count = lax.axis_size("ctx")
    exp_count = lax.axis_size("exp")
    _, rows_q, heads, width = queries.shape
    rows_k = latent_keys.shape[1]
    share = rows_k // exp_count
    keys_all = rows_k * ctx_count
    rows_all = rows_q * heads
    both = width + LATENT

    def f32(*shape):
        return jax.ShapeDtypeStruct(shape, F32)

    def bf16(*shape):
        return jax.ShapeDtypeStruct(shape, BF16)

    own_keys = latent_keys[0].T
    peer_keys = [shift(own_keys, "ctx", b) for b in range(1, ctx_count)]

    *prepared, query_pos, kv_gain_row = call(
        fetch_kernel,
        [
            bf16(width, rows_all),
            bf16(rows_all, LATENT),
            bf16(rows_k, width),
            jax.ShapeDtypeStruct((1, rows_all), jnp.int32),
            f32(1, LATENT),
        ],
        [
            query_groups,
            kv_gain.reshape(1, LATENT),
            jnp.transpose(queries[0], (1, 2, 0)),
            out_grad[0],
            own_keys,
        ],
        rows_all * width,
        [
            pltpu.SMEM(query_groups.shape, jnp.int32),
            pltpu.VMEM((rows_q, heads, LATENT), BF16),
            pltpu.VMEM((width, rows_k), BF16),
            pltpu.SemaphoreType.DMA((4 + heads,)),
        ],
        fetch=True,
    )
    dscore, own, gain, *sends = call(
        lambda *refs: softmax_kernel(ctx_count, *refs),
        [bf16(keys_all, rows_all), f32(exp_count, share, width), f32(1, LATENT)]
        + [bf16(exp_count, share, width + TAIL)] * (ctx_count - 1),
        [*prepared, query_pos, *peer_keys],
        4 * rows_all * keys_all * both,
    )
    received = [shift(sends[b - 1], "ctx", -b) for b in range(1, ctx_count)]
    dq_t, mark = call(
        grad_queries_kernel,
        [bf16(heads, width, rows_q), f32(1, 128)],
        [dscore, own_keys, *peer_keys],
        2 * rows_all * keys_all * width,
    )
    message = bf16(max(share, 2 * TAIL_ROWS), width + TAIL)
    mesh_shape = (lax.axis_size("dp"), ctx_count, exp_count)
    steps = exp_pairs(mesh_shape)
    kept, gain, *sends = call(
        lambda *refs: pair_kernel(mesh_shape, *refs),
        [f32(share, width), f32(1, LATENT)] + [message] * len(steps),
        [own, gain, *received],
        rows_k * width * ctx_count,
    )
    received = [send_step(send, step) for send, step in zip(sends, steps)]
    (gain,) = call(gain_kernel, [f32(1, LATENT)], [gain, mark, *received], LATENT * exp_count)

    gains = [send_step(gain, step) for step in reversed(dp_pairs(mesh_shape))]
    (grad_keys,) = call(
        rows_kernel, [f32(share, width)], [gain, kept, *received], share * width * exp_count
    )
    (grad_gain,) = call(
        final_kernel, [f32(1, LATENT)], [kv_gain_row, gain, *gains], LATENT * len(gains)
    )
    grad_queries = jnp.transpose(dq_t, (2, 0, 1))[None]
    return (grad_queries, grad_keys[None, None], grad_gain.reshape(LATENT))


def solution(mesh):
    in_specs = (
        P("dp", "ctx", "exp", None),
        P("dp", "ctx", "exp", None),
        P("dp", "ctx", None),
        P(),
        P("dp", None),
    )
    out_specs = (P("dp", "ctx", "exp", None), P("dp", "ctx", "exp", None), P())
    return jax.shard_map(body, mesh=mesh, in_specs=in_specs, out_specs=out_specs, check_vma=False)
```

```python
import math

import jax
import jax.numpy as jnp
from jax import lax
from jax.experimental import pallas as pl
from jax.experimental.pallas import tpu as pltpu
from jax.sharding import PartitionSpec as P

LATENT = 512
SOFTMAX_SCALE = (0.1 * math.log(40.0) + 1.0) ** 2 / math.sqrt(192.0)
MASKED_SCORE = -1e30
TAIL = 64
TAIL_ROWS = LATENT // TAIL

NT = (((1,), (1,)), ((), ()))
F32, BF16 = jnp.float32, jnp.bfloat16


def shift(value, axis, step):
    size = lax.axis_size(axis)
    return lax.ppermute(value, axis, [(i, (i - step) % size) for i in range(size)])


EXP_STEPS = (
    ((4, 5, 0, 7, 6, 1, 2, 3), (1, 2, 3, 0, 5, 7, 4, 6), (3, 0, 1, 2, 7, 6, 5, 4), (2, 3, 6, 1, 0, 4, 7, 5)),
    ((4, 5, 0, 7, 6, 1, 2, 3), (1, 2, 3, 0, 5, 7, 4, 6), (3, 0, 1, 2, 7, 6, 5, 4), (2, 3, 6, 1, 0, 4, 7, 5)),
    ((4, 5, 0, 7, 6, 1, 2, 3), (1, 2, 3, 0, 5, 7, 4, 6), (3, 0, 1, 2, 7, 6, 5, 4), (2, 3, 6, 1, 0, 4, 7, 5)),
    ((4, 5, 0, 7, 6, 1, 2, 3), (1, 2, 3, 0, 5, 7, 4, 6), (3, 0, 1, 2, 7, 6, 5, 4), (2, 3, 6, 1, 0, 4, 7, 5)),
)
DP_STEPS = (
    (
        (4, 5, 6, 7, 2, 1, 0, 3),
        (1, 2, 5, 0, 3, 6, 7, 4),
        (7, 3, 1, 2, 5, 0, 4, 6),
        (6, 7, 3, 1, 0, 4, 2, 5),
    ),
    (
        (3, 6, 5, 0, 7, 2, 1, 4),
        (6, 3, 7, 5, 1, 4, 0, 2),
        (2, 7, 3, 1, 5, 0, 4, 6),
        (4, 5, 6, 7, 0, 1, 2, 3),
    ),
    (
        (7, 6, 5, 4, 2, 3, 0, 1),
        (6, 7, 1, 5, 3, 2, 4, 0),
        (5, 0, 7, 6, 1, 4, 3, 2),
        (4, 5, 6, 7, 0, 1, 2, 3),
    ),
    (
        (7, 0, 5, 1, 2, 6, 3, 4),
        (5, 7, 0, 2, 1, 3, 4, 6),
        (3, 4, 1, 5, 6, 2, 7, 0),
        (4, 5, 6, 7, 0, 1, 2, 3),
    ),
)


def ring_steps(size):
    return tuple(tuple((i + k) % size for i in range(size)) for k in range(1, size))


def tuned(mesh_shape):
    return mesh_shape == (4, 2, 4)


def exp_pairs(mesh_shape):
    dp_count, ctx_count, exp_count = mesh_shape
    if tuned(mesh_shape):
        return [
            [
                (d * 8 + k, d * 8 + to)
                for d in range(dp_count)
                for k, to in enumerate(EXP_STEPS[d][i])
            ]
            for i in range(len(EXP_STEPS[0]))
        ]
    return [
        [
            (group * exp_count + i, group * exp_count + to)
            for group in range(dp_count * ctx_count)
            for i, to in enumerate(step)
        ]
        for step in ring_steps(exp_count)
    ]


def dp_pairs(mesh_shape):
    dp_count, ctx_count, exp_count = mesh_shape
    if tuned(mesh_shape):
        return [
            [
                (k % 4 * 8 + k // 4 * 4 + z, to % 4 * 8 + to // 4 * 4 + z)
                for z in range(exp_count)
                for k, to in enumerate(DP_STEPS[z][i])
            ]
            for i in range(len(DP_STEPS[0]))
        ]
    size = ctx_count * exp_count
    return [
        [(i * size + j, to * size + j) for i, to in enumerate(step) for j in range(size)]
        for step in ring_steps(dp_count)
    ]


def exp_target(mesh_shape, index):
    exp_count = mesh_shape[2]
    place = lax.axis_index("exp")
    if not tuned(mesh_shape):
        return lax.rem(place + ring_steps(exp_count)[index][0], exp_count), True
    core, row = lax.axis_index("ctx"), lax.axis_index("dp")
    words = [sum(to << 3 * k for k, to in enumerate(column[index])) for column in EXP_STEPS]
    word = jnp.int32(words[0])
    for i in range(1, len(words)):
        word = jnp.where(row == i, words[i], word)
    target = (word >> (3 * (core * 4 + place))) & 7
    return target & 3, (target >> 2) == core


def dp_counts(mesh_shape, index):
    if not tuned(mesh_shape):
        return True
    word = 0
    for source, to in dp_pairs(mesh_shape)[index]:
        word |= (source // 8 != to // 8) << to
    place = (lax.axis_index("dp") * 2 + lax.axis_index("ctx")) * 4 + lax.axis_index("exp")
    return (jnp.int32(word - (word >> 31 << 32)) >> place) & 1 == 1


def send_step(value, pairs):
    return lax.ppermute(value, ("dp", "ctx", "exp"), pairs)


def dot(a, b):
    return jnp.dot(a, b, preferred_element_type=F32)


def dot_nt(a, b):
    return lax.dot_general(a, b, NT, preferred_element_type=F32)


def gain_tail(gain):
    high = gain.astype(BF16).astype(F32)
    return jnp.concatenate(
        [
            part[:, r * TAIL : (r + 1) * TAIL]
            for part in (high, gain - high)
            for r in range(TAIL_ROWS)
        ],
        axis=0,
    ).astype(BF16)


def tail_gain(tail):
    tail = tail[:TAIL_ROWS] + tail[TAIL_ROWS:]
    return jnp.concatenate([tail[r : r + 1] for r in range(TAIL_ROWS)], axis=1)


def write_tail(ref, tail):
    rows, width = ref.shape
    if rows > 2 * TAIL_ROWS:
        ref[2 * TAIL_ROWS :, width - TAIL :] = jnp.zeros((rows - 2 * TAIL_ROWS, TAIL), BF16)
    ref[: 2 * TAIL_ROWS, width - TAIL :] = tail


def tail_blocks(share):
    step = min(share, 2 * TAIL_ROWS)
    return [(j, slice(j * step, (j + 1) * step), step) for j in range(2 * TAIL_ROWS // step)]


def fetch_kernel(
    groups_hbm, kv_gain_hbm, q_hbm, g_hbm, key_hbm,
    queries_ref, grads_ref, keys_ref, query_pos_ref, kv_gain_ref,
    groups, g_ref, key_ref, copied,
):
    heads, _, rows_q = q_hbm.shape
    q_copies = [
        pltpu.make_async_copy(
            q_hbm.at[h], queries_ref.at[:, pl.ds(h * rows_q, rows_q)], copied.at[4 + h]
        )
        for h in range(heads)
    ]
    key_copy = pltpu.make_async_copy(key_hbm, key_ref, copied.at[0])
    groups_copy = pltpu.make_async_copy(groups_hbm, groups, copied.at[1])
    g_copy = pltpu.make_async_copy(g_hbm, g_ref, copied.at[2])
    gain_copy = pltpu.make_async_copy(kv_gain_hbm, kv_gain_ref, copied.at[3])
    for copy in (g_copy, key_copy, groups_copy, *q_copies, gain_copy):
        copy.start()

    g_copy.wait()
    grads_ref[...] = jnp.swapaxes(g_ref[...], 0, 1).reshape(heads * rows_q, LATENT)
    key_copy.wait()
    keys_ref[...] = key_ref[...].T
    groups_copy.wait()
    query_pos_ref[...] = groups[0, lax.axis_index("ctx")] * rows_q + lax.rem(
        lax.broadcasted_iota(jnp.int32, (1, heads * rows_q), 1), rows_q
    )
    for copy in (*q_copies, gain_copy):
        copy.wait()


def softmax_kernel(ctx_count, *refs):
    queries_ref, grads_ref, keys_ref, query_pos_ref = refs[:4]
    peer_refs = refs[4 : 3 + ctx_count]
    dscore_ref, own_ref, gain_ref = refs[3 + ctx_count : 6 + ctx_count]
    send_refs = refs[6 + ctx_count :]
    rows_k = keys_ref.shape[0]
    place = lax.axis_index("ctx")
    queries_t = queries_ref[...]
    grads = grads_ref[...]
    query_pos = query_pos_ref[...]

    keys = jnp.concatenate([keys_ref[...]] + [ref[...].T for ref in peer_refs], axis=0)
    scores = dot(keys, queries_t) * SOFTMAX_SCALE
    grad_prob = dot_nt(keys[:, :LATENT], grads)
    key_row = lax.broadcasted_iota(jnp.int32, (rows_k, scores.shape[1]), 0)
    visible = jnp.concatenate(
        [key_row + lax.rem(place + b, ctx_count) * rows_k <= query_pos for b in range(ctx_count)],
        axis=0,
    )
    scores = jnp.where(visible, scores, MASKED_SCORE)
    row_max = jnp.max(scores, axis=0, keepdims=True)
    exponent = jnp.exp(scores - row_max)
    weights = exponent * (1.0 / jnp.sum(exponent, axis=0, keepdims=True))
    row_delta = jnp.sum(weights * grad_prob, axis=0, keepdims=True)
    dscore = (weights * (grad_prob - row_delta)).astype(BF16)
    weights_low = weights.astype(BF16)
    dscore_ref[...] = dscore

    key_part = dot_nt(dscore, queries_t) * SOFTMAX_SCALE
    latent_part = key_part[:, :LATENT] + dot(weights_low, grads)
    gain = jnp.sum(latent_part * keys[:, :LATENT].astype(F32), axis=0, keepdims=True)
    gain_ref[...] = gain
    tail = gain_tail(gain)
    blocks, share, width = own_ref.shape
    for b in range(ctx_count):
        rows = slice(b * rows_k, (b + 1) * rows_k)
        target = own_ref if b == 0 else send_refs[b - 1]
        latent_rows = latent_part[rows].reshape(blocks, share, LATENT)
        rope_rows = key_part[rows, LATENT:].reshape(blocks, share, width - LATENT)
        target[:, :, :LATENT] = latent_rows.astype(target.dtype)
        target[:, :, LATENT:width] = rope_rows.astype(target.dtype)
        if b:
            target[:, :, width:] = jnp.zeros((blocks, share, TAIL), BF16)
            for j, part, step in tail_blocks(share):
                target[j, :step, width:] = tail[part]


def grad_queries_kernel(*refs):
    dscore_ref, *key_refs, dq_ref, mark_ref = refs
    mark_ref[...] = jnp.zeros(mark_ref.shape, F32)
    heads, _, rows_q = dq_ref.shape
    keys_t = jnp.concatenate([ref[...] for ref in key_refs], axis=1)
    dq_t = dot(keys_t, dscore_ref[...]) * SOFTMAX_SCALE
    for h in range(heads):
        dq_ref[h] = dq_t[:, h * rows_q : (h + 1) * rows_q].astype(BF16)


def pair_kernel(mesh_shape, *refs):
    ctx_count = mesh_shape[1]
    own_ref, gain_ref = refs[:2]
    recv_refs = refs[2 : 1 + ctx_count]
    kept_ref, gain_out = refs[1 + ctx_count : 3 + ctx_count]
    send_refs = refs[3 + ctx_count :]
    share, width = own_ref.shape[1:]

    def block(i):
        rows = own_ref[i]
        for ref in recv_refs:
            rows = rows + ref[i, :, :width].astype(F32)
        return rows

    gain = gain_ref[...]
    for ref in recv_refs:
        tail = [ref[j, :step, width:] for j, _, step in tail_blocks(share)]
        gain = gain + tail_gain(jnp.concatenate(tail, axis=0).astype(F32))
    gain_out[...] = gain
    tail = gain_tail(gain)
    kept_ref[...] = block(lax.axis_index("exp"))
    for index, ref in enumerate(send_refs):
        target, sends = exp_target(mesh_shape, index)
        if ref.shape[0] > share:
            ref[...] = jnp.zeros(ref.shape, ref.dtype)
        rows = block(target)
        ref[:share, :width] = jnp.where(sends, rows, jnp.zeros_like(rows)).astype(BF16)
        write_tail(ref, jnp.where(sends, tail, jnp.zeros_like(tail)))


def gain_kernel(*refs):
    gain_ref, _, *recv_refs, gain_out = refs
    tail = jnp.zeros((2 * TAIL_ROWS, TAIL), F32)
    for ref in recv_refs:
        tail = tail + ref[: 2 * TAIL_ROWS, ref.shape[1] - TAIL :].astype(F32)
    gain_out[...] = gain_ref[...] + tail_gain(tail)


def rows_kernel(*refs):
    _, kept_ref, *recv_refs, out_ref = refs
    share, width = kept_ref.shape
    rows = kept_ref[...]
    for ref in recv_refs:
        rows = rows + ref[:share, :width].astype(F32)
    out_ref[...] = rows


def final_kernel(mesh_shape, *refs):
    kv_gain_ref, gain_ref, *recv_refs, gain_out = refs
    gain = gain_ref[...]
    for index, ref in enumerate(reversed(recv_refs)):
        heard = ref[...]
        gain = gain + jnp.where(dp_counts(mesh_shape, index), heard, jnp.zeros_like(heard))
    gain_out[...] = gain / kv_gain_ref[...]


def call(kernel, out_shapes, operands, flops, scratch=(), fetch=False):
    space = pl.ANY if fetch else pltpu.VMEM
    size = sum(x.size * x.dtype.itemsize for x in (*operands, *out_shapes))
    if fetch:
        out_shapes = [pltpu.VMEM(x.shape, x.dtype) for x in out_shapes]
    return pl.pallas_call(
        kernel,
        out_shape=list(out_shapes),
        in_specs=[pl.BlockSpec(memory_space=space)] * len(operands),
        out_specs=[pl.BlockSpec(memory_space=pltpu.VMEM)] * len(out_shapes),
        scratch_shapes=list(scratch),
        compiler_params=pltpu.CompilerParams(vmem_limit_bytes=(56 if fetch else 48) * 2**20),
        cost_estimate=pl.CostEstimate(flops=flops, bytes_accessed=size, transcendentals=0),
    )(*operands)


def body(queries, out_grad, latent_keys, kv_gain, query_groups):
    ctx_count = lax.axis_size("ctx")
    exp_count = lax.axis_size("exp")
    _, rows_q, heads, width = queries.shape
    rows_k = latent_keys.shape[1]
    share = rows_k // exp_count
    keys_all = rows_k * ctx_count
    rows_all = rows_q * heads
    both = width + LATENT

    def f32(*shape):
        return jax.ShapeDtypeStruct(shape, F32)

    def bf16(*shape):
        return jax.ShapeDtypeStruct(shape, BF16)

    own_keys = latent_keys[0].T
    peer_keys = [shift(own_keys, "ctx", b) for b in range(1, ctx_count)]

    *prepared, query_pos, kv_gain_row = call(
        fetch_kernel,
        [
            bf16(width, rows_all),
            bf16(rows_all, LATENT),
            bf16(rows_k, width),
            jax.ShapeDtypeStruct((1, rows_all), jnp.int32),
            f32(1, LATENT),
        ],
        [
            query_groups,
            kv_gain.reshape(1, LATENT),
            jnp.transpose(queries[0], (1, 2, 0)),
            out_grad[0],
            own_keys,
        ],
        rows_all * width,
        [
            pltpu.SMEM(query_groups.shape, jnp.int32),
            pltpu.VMEM((rows_q, heads, LATENT), BF16),
            pltpu.VMEM((width, rows_k), BF16),
            pltpu.SemaphoreType.DMA((4 + heads,)),
        ],
        fetch=True,
    )
    dscore, own, gain, *sends = call(
        lambda *refs: softmax_kernel(ctx_count, *refs),
        [bf16(keys_all, rows_all), f32(exp_count, share, width), f32(1, LATENT)]
        + [bf16(exp_count, share, width + TAIL)] * (ctx_count - 1),
        [*prepared, query_pos, *peer_keys],
        4 * rows_all * keys_all * both,
    )
    received = [shift(sends[b - 1], "ctx", -b) for b in range(1, ctx_count)]
    dq_t, mark = call(
        grad_queries_kernel,
        [bf16(heads, width, rows_q), f32(1, 128)],
        [dscore, own_keys, *peer_keys],
        2 * rows_all * keys_all * width,
    )
    message = bf16(max(share, 2 * TAIL_ROWS), width + TAIL)
    mesh_shape = (lax.axis_size("dp"), ctx_count, exp_count)
    steps = exp_pairs(mesh_shape)
    kept, gain, *sends = call(
        lambda *refs: pair_kernel(mesh_shape, *refs),
        [f32(share, width), f32(1, LATENT)] + [message] * len(steps),
        [own, gain, *received],
        rows_k * width * ctx_count,
    )
    received = [send_step(send, step) for send, step in zip(sends, steps)]
    (gain,) = call(gain_kernel, [f32(1, LATENT)], [gain, mark, *received], LATENT * exp_count)

    gains = [send_step(gain, step) for step in reversed(dp_pairs(mesh_shape))]
    (grad_keys,) = call(
        rows_kernel, [f32(share, width)], [gain, kept, *received], share * width * exp_count
    )
    (grad_gain,) = call(
        lambda *refs: final_kernel(mesh_shape, *refs),
        [f32(1, LATENT)],
        [kv_gain_row, gain, *gains],
        LATENT * len(gains),
    )
    grad_queries = jnp.transpose(dq_t, (2, 0, 1))[None]
    return (grad_queries, grad_keys[None, None], grad_gain.reshape(LATENT))


def solution(mesh):
    in_specs = (
        P("dp", "ctx", "exp", None),
        P("dp", "ctx", "exp", None),
        P("dp", "ctx", None),
        P(),
        P("dp", None),
    )
    out_specs = (P("dp", "ctx", "exp", None), P("dp", "ctx", "exp", None), P())
    return jax.shard_map(body, mesh=mesh, in_specs=in_specs, out_specs=out_specs, check_vma=False)
```

```python
import math

import jax
import jax.numpy as jnp
from jax import lax
from jax.experimental import pallas as pl
from jax.experimental.pallas import tpu as pltpu
from jax.sharding import PartitionSpec as P

LATENT = 512
SOFTMAX_SCALE = (0.1 * math.log(40.0) + 1.0) ** 2 / math.sqrt(192.0)
MASKED_SCORE = -1e30
TAIL = 64
TAIL_ROWS = LATENT // TAIL

NT = (((1,), (1,)), ((), ()))
F32, BF16 = jnp.float32, jnp.bfloat16


def shift(value, axis, step):
    size = lax.axis_size(axis)
    return lax.ppermute(value, axis, [(i, (i - step) % size) for i in range(size)])


EXP_STEPS = (
    ((4, 5, 0, 7, 6, 1, 2, 3), (1, 2, 3, 0, 5, 7, 4, 6), (3, 0, 1, 2, 7, 6, 5, 4), (2, 3, 6, 1, 0, 4, 7, 5)),
    ((4, 5, 0, 7, 6, 1, 2, 3), (1, 2, 3, 0, 5, 7, 4, 6), (3, 0, 1, 2, 7, 6, 5, 4), (2, 3, 6, 1, 0, 4, 7, 5)),
    ((4, 5, 0, 7, 6, 1, 2, 3), (1, 2, 3, 0, 5, 7, 4, 6), (3, 0, 1, 2, 7, 6, 5, 4), (2, 3, 6, 1, 0, 4, 7, 5)),
    ((4, 5, 0, 7, 6, 1, 2, 3), (1, 2, 3, 0, 5, 7, 4, 6), (3, 0, 1, 2, 7, 6, 5, 4), (2, 3, 6, 1, 0, 4, 7, 5)),
)
DP_STEPS = (
    ((1, 2, 7, 6, 3, 0, 5, 4), (5, 3, 1, 2, 7, 6, 4, 0), (6, 7, 3, 1, 2, 4, 0, 5)),
    ((6, 2, 5, 0, 7, 3, 1, 4), (5, 6, 7, 1, 3, 0, 4, 2), (2, 7, 3, 5, 1, 4, 0, 6)),
    ((6, 7, 0, 1, 2, 3, 5, 4), (7, 6, 3, 0, 1, 2, 4, 5), (5, 0, 7, 6, 3, 4, 1, 2)),
    ((6, 3, 5, 0, 2, 7, 1, 4), (7, 4, 0, 2, 5, 6, 3, 1), (3, 0, 4, 6, 1, 2, 7, 5)),
)


def ring_steps(size):
    return tuple(tuple((i + k) % size for i in range(size)) for k in range(1, size))


def tuned(mesh_shape):
    return mesh_shape == (4, 2, 4)


def exp_pairs(mesh_shape):
    dp_count, ctx_count, exp_count = mesh_shape
    if tuned(mesh_shape):
        return [
            [
                (d * 8 + k, d * 8 + to)
                for d in range(dp_count)
                for k, to in enumerate(EXP_STEPS[d][i])
            ]
            for i in range(len(EXP_STEPS[0]))
        ]
    return [
        [
            (group * exp_count + i, group * exp_count + to)
            for group in range(dp_count * ctx_count)
            for i, to in enumerate(step)
        ]
        for step in ring_steps(exp_count)
    ]


def dp_pairs(mesh_shape):
    dp_count, ctx_count, exp_count = mesh_shape
    if tuned(mesh_shape):
        return [
            [
                (k % 4 * 8 + k // 4 * 4 + z, to % 4 * 8 + to // 4 * 4 + z)
                for z in range(exp_count)
                for k, to in enumerate(DP_STEPS[z][i])
            ]
            for i in range(len(DP_STEPS[0]))
        ]
    size = ctx_count * exp_count
    return [
        [(i * size + j, to * size + j) for i, to in enumerate(step) for j in range(size)]
        for step in ring_steps(dp_count)
    ]


def exp_target(mesh_shape, index):
    exp_count = mesh_shape[2]
    place = lax.axis_index("exp")
    if not tuned(mesh_shape):
        return lax.rem(place + ring_steps(exp_count)[index][0], exp_count), True
    core, row = lax.axis_index("ctx"), lax.axis_index("dp")
    words = [sum(to << 3 * k for k, to in enumerate(column[index])) for column in EXP_STEPS]
    word = jnp.int32(words[0])
    for i in range(1, len(words)):
        word = jnp.where(row == i, words[i], word)
    target = (word >> (3 * (core * 4 + place))) & 7
    return target & 3, (target >> 2) == core


def send_step(value, pairs):
    return lax.ppermute(value, ("dp", "ctx", "exp"), pairs)


def dot(a, b):
    return jnp.dot(a, b, preferred_element_type=F32)


def dot_nt(a, b):
    return lax.dot_general(a, b, NT, preferred_element_type=F32)


def gain_tail(gain):
    high = gain.astype(BF16).astype(F32)
    return jnp.concatenate(
        [
            part[:, r * TAIL : (r + 1) * TAIL]
            for part in (high, gain - high)
            for r in range(TAIL_ROWS)
        ],
        axis=0,
    ).astype(BF16)


def tail_gain(tail):
    tail = tail[:TAIL_ROWS] + tail[TAIL_ROWS:]
    return jnp.concatenate([tail[r : r + 1] for r in range(TAIL_ROWS)], axis=1)


def write_tail(ref, tail):
    rows, width = ref.shape
    if rows > 2 * TAIL_ROWS:
        ref[2 * TAIL_ROWS :, width - TAIL :] = jnp.zeros((rows - 2 * TAIL_ROWS, TAIL), BF16)
    ref[: 2 * TAIL_ROWS, width - TAIL :] = tail


def tail_blocks(share):
    step = min(share, 2 * TAIL_ROWS)
    return [(j, slice(j * step, (j + 1) * step), step) for j in range(2 * TAIL_ROWS // step)]


def fetch_kernel(
    groups_hbm, kv_gain_hbm, q_hbm, g_hbm, key_hbm,
    queries_ref, grads_ref, keys_ref, query_pos_ref, kv_gain_ref,
    groups, g_ref, key_ref, copied,
):
    heads, _, rows_q = q_hbm.shape
    q_copy = pltpu.make_async_copy(q_hbm, queries_ref, copied.at[4])
    key_copy = pltpu.make_async_copy(key_hbm, key_ref, copied.at[0])
    groups_copy = pltpu.make_async_copy(groups_hbm, groups, copied.at[1])
    g_copy = pltpu.make_async_copy(g_hbm, g_ref, copied.at[2])
    gain_copy = pltpu.make_async_copy(kv_gain_hbm, kv_gain_ref, copied.at[3])
    for copy in (g_copy, key_copy, groups_copy, q_copy, gain_copy):
        copy.start()

    g_copy.wait()
    grads_ref[...] = jnp.swapaxes(g_ref[...], 0, 1).reshape(heads * rows_q, LATENT)
    key_copy.wait()
    keys_ref[...] = key_ref[...].T
    groups_copy.wait()
    query_pos_ref[...] = groups[0, lax.axis_index("ctx")] * rows_q + lax.rem(
        lax.broadcasted_iota(jnp.int32, (1, heads * rows_q), 1), rows_q
    )
    q_copy.wait()
    gain_copy.wait()


def softmax_kernel(ctx_count, *refs):
    queries_ref, grads_ref, keys_ref, query_pos_ref = refs[:4]
    peer_refs = refs[4 : 3 + ctx_count]
    dscore_ref, own_ref, gain_ref = refs[3 + ctx_count : 6 + ctx_count]
    send_refs = refs[6 + ctx_count :]
    rows_k = keys_ref.shape[0]
    place = lax.axis_index("ctx")
    queries_t = jnp.concatenate([queries_ref[h] for h in range(queries_ref.shape[0])], axis=1)
    grads = grads_ref[...]
    query_pos = query_pos_ref[...]

    keys = jnp.concatenate([keys_ref[...]] + [ref[...].T for ref in peer_refs], axis=0)
    scores = dot(keys, queries_t)
    grad_prob = dot_nt(keys[:, :LATENT], grads)
    key_row = lax.broadcasted_iota(jnp.int32, (rows_k, scores.shape[1]), 0)
    visible = jnp.concatenate(
        [key_row + lax.rem(place + b, ctx_count) * rows_k <= query_pos for b in range(ctx_count)],
        axis=0,
    )
    scores = jnp.where(visible, scores, MASKED_SCORE)
    row_max = jnp.max(scores, axis=0, keepdims=True)
    exponent = jnp.exp2((scores - row_max) * (SOFTMAX_SCALE * math.log2(math.e)))
    inverse = 1.0 / jnp.sum(exponent, axis=0, keepdims=True)
    row_delta = jnp.sum(exponent * grad_prob, axis=0, keepdims=True) * inverse
    weights = exponent * inverse
    dscore = (weights * (grad_prob - row_delta)).astype(BF16)
    weights_low = weights.astype(BF16)
    dscore_ref[...] = dscore

    key_part = dot_nt(dscore, queries_t) * SOFTMAX_SCALE
    latent_part = key_part[:, :LATENT] + dot(weights_low, grads)
    gain = jnp.sum(latent_part * keys[:, :LATENT].astype(F32), axis=0, keepdims=True)
    gain_ref[...] = gain
    tail = gain_tail(gain)
    blocks, share, width = own_ref.shape
    for b in range(ctx_count):
        rows = slice(b * rows_k, (b + 1) * rows_k)
        target = own_ref if b == 0 else send_refs[b - 1]
        latent_rows = latent_part[rows].reshape(blocks, share, LATENT)
        rope_rows = key_part[rows, LATENT:].reshape(blocks, share, width - LATENT)
        target[:, :, :LATENT] = latent_rows.astype(target.dtype)
        target[:, :, LATENT:width] = rope_rows.astype(target.dtype)
        if b:
            target[:, :, width:] = jnp.zeros((blocks, share, TAIL), BF16)
            for j, part, step in tail_blocks(share):
                target[j, :step, width:] = tail[part]


def grad_queries_kernel(*refs):
    dscore_ref, *key_refs, dq_ref, mark_ref = refs
    mark_ref[...] = jnp.zeros(mark_ref.shape, F32)
    heads, _, rows_q = dq_ref.shape
    keys_t = jnp.concatenate([ref[...] for ref in key_refs], axis=1)
    dq_t = dot(keys_t, dscore_ref[...]) * SOFTMAX_SCALE
    for h in range(heads):
        dq_ref[h] = dq_t[:, h * rows_q : (h + 1) * rows_q].astype(BF16)


def pair_kernel(mesh_shape, *refs):
    ctx_count = mesh_shape[1]
    own_ref, gain_ref = refs[:2]
    recv_refs = refs[2 : 1 + ctx_count]
    kept_ref, gain_out = refs[1 + ctx_count : 3 + ctx_count]
    send_refs = refs[3 + ctx_count :]
    share, width = own_ref.shape[1:]

    def block(i):
        rows = own_ref[i]
        for ref in recv_refs:
            rows = rows + ref[i, :, :width].astype(F32)
        return rows

    gain = gain_ref[...]
    for ref in recv_refs:
        tail = [ref[j, :step, width:] for j, _, step in tail_blocks(share)]
        gain = gain + tail_gain(jnp.concatenate(tail, axis=0).astype(F32))
    gain_out[...] = gain
    tail = gain_tail(gain)
    kept_ref[...] = block(lax.axis_index("exp"))
    for index, ref in enumerate(send_refs):
        target, sends = exp_target(mesh_shape, index)
        if ref.shape[0] > share:
            ref[...] = jnp.zeros(ref.shape, ref.dtype)
        rows = block(target)
        ref[:share, :width] = jnp.where(sends, rows, jnp.zeros_like(rows)).astype(BF16)
        write_tail(ref, jnp.where(sends, tail, jnp.zeros_like(tail)))


def gain_kernel(*refs):
    gain_ref, _, *recv_refs, gain_out = refs
    tail = jnp.zeros((2 * TAIL_ROWS, TAIL), F32)
    for ref in recv_refs:
        tail = tail + ref[: 2 * TAIL_ROWS, ref.shape[1] - TAIL :].astype(F32)
    gain_out[...] = gain_ref[...] + tail_gain(tail)


def rows_kernel(*refs):
    _, kept_ref, *recv_refs, out_ref = refs
    share, width = kept_ref.shape
    rows = kept_ref[...]
    for ref in recv_refs:
        rows = rows + ref[:share, :width].astype(F32)
    out_ref[...] = rows


def final_kernel(*refs):
    kv_gain_ref, gain_ref, *recv_refs, gain_out = refs
    gain = gain_ref[...]
    for ref in recv_refs:
        gain = gain + ref[...]
    gain_out[...] = gain / kv_gain_ref[...]


def call(kernel, out_shapes, operands, flops, scratch=(), fetch=False):
    space = pl.ANY if fetch else pltpu.VMEM
    size = sum(x.size * x.dtype.itemsize for x in (*operands, *out_shapes))
    if fetch:
        out_shapes = [pltpu.VMEM(x.shape, x.dtype) for x in out_shapes]
    return pl.pallas_call(
        kernel,
        out_shape=list(out_shapes),
        in_specs=[pl.BlockSpec(memory_space=space)] * len(operands),
        out_specs=[pl.BlockSpec(memory_space=pltpu.VMEM)] * len(out_shapes),
        scratch_shapes=list(scratch),
        compiler_params=pltpu.CompilerParams(vmem_limit_bytes=(56 if fetch else 48) * 2**20),
        cost_estimate=pl.CostEstimate(flops=flops, bytes_accessed=size, transcendentals=0),
    )(*operands)


def body(queries, out_grad, latent_keys, kv_gain, query_groups):
    ctx_count = lax.axis_size("ctx")
    exp_count = lax.axis_size("exp")
    _, rows_q, heads, width = queries.shape
    rows_k = latent_keys.shape[1]
    share = rows_k // exp_count
    keys_all = rows_k * ctx_count
    rows_all = rows_q * heads
    both = width + LATENT

    def f32(*shape):
        return jax.ShapeDtypeStruct(shape, F32)

    def bf16(*shape):
        return jax.ShapeDtypeStruct(shape, BF16)

    own_keys = latent_keys[0].T
    peer_keys = [shift(own_keys, "ctx", b) for b in range(1, ctx_count)]

    *prepared, query_pos, kv_gain_row = call(
        fetch_kernel,
        [
            bf16(heads, width, rows_q),
            bf16(rows_all, LATENT),
            bf16(rows_k, width),
            jax.ShapeDtypeStruct((1, rows_all), jnp.int32),
            f32(1, LATENT),
        ],
        [
            query_groups,
            kv_gain.reshape(1, LATENT),
            jnp.transpose(queries[0], (1, 2, 0)),
            out_grad[0],
            own_keys,
        ],
        rows_all * width,
        [
            pltpu.SMEM(query_groups.shape, jnp.int32),
            pltpu.VMEM((rows_q, heads, LATENT), BF16),
            pltpu.VMEM((width, rows_k), BF16),
            pltpu.SemaphoreType.DMA((5,)),
        ],
        fetch=True,
    )
    dscore, own, gain, *sends = call(
        lambda *refs: softmax_kernel(ctx_count, *refs),
        [bf16(keys_all, rows_all), f32(exp_count, share, width), f32(1, LATENT)]
        + [bf16(exp_count, share, width + TAIL)] * (ctx_count - 1),
        [*prepared, query_pos, *peer_keys],
        4 * rows_all * keys_all * both,
    )
    received = [shift(sends[b - 1], "ctx", -b) for b in range(1, ctx_count)]
    dq_t, mark = call(
        grad_queries_kernel,
        [bf16(heads, width, rows_q), f32(1, 128)],
        [dscore, own_keys, *peer_keys],
        2 * rows_all * keys_all * width,
    )
    message = bf16(max(share, 2 * TAIL_ROWS), width + TAIL)
    mesh_shape = (lax.axis_size("dp"), ctx_count, exp_count)
    steps = exp_pairs(mesh_shape)
    kept, gain, *sends = call(
        lambda *refs: pair_kernel(mesh_shape, *refs),
        [f32(share, width), f32(1, LATENT)] + [message] * len(steps),
        [own, gain, *received],
        rows_k * width * ctx_count,
    )
    received = [send_step(send, step) for send, step in zip(sends, steps)]
    (gain,) = call(gain_kernel, [f32(1, LATENT)], [gain, mark, *received], LATENT * exp_count)

    gains = [send_step(gain, step) for step in reversed(dp_pairs(mesh_shape))]
    (grad_keys,) = call(
        rows_kernel, [f32(share, width)], [gain, kept, *received], share * width * exp_count
    )
    (grad_gain,) = call(
        final_kernel, [f32(1, LATENT)], [kv_gain_row, gain, *gains], LATENT * len(gains)
    )
    grad_queries = jnp.transpose(dq_t, (2, 0, 1))[None]
    return (grad_queries, grad_keys[None, None], grad_gain.reshape(LATENT))


def solution(mesh):
    in_specs = (
        P("dp", "ctx", "exp", None),
        P("dp", "ctx", "exp", None),
        P("dp", "ctx", None),
        P(),
        P("dp", None),
    )
    out_specs = (P("dp", "ctx", "exp", None), P("dp", "ctx", "exp", None), P())
    return jax.shard_map(body, mesh=mesh, in_specs=in_specs, out_specs=out_specs, check_vma=False)
```
